32 devices in a mesh: pw: 8 (over z, y), band: 4 (over x, core).
Axes of the slice: x: 2, y: 2, z: 4, core: 2. Of those that a mesh axis runs over, the one named last changes fastest.
Arguments:
- residual_directions: float32 [2, 512, 4, 2048], P(None, 'pw', 'band'), may hold values from -6 to 6
- local_field_applied: float32 [2, 512, 4, 2048], P(None, 'pw', 'band'), may hold values from -6 to 6
- orbital_running_sum: bfloat16 [2, 2048, 4, 2048], P(None, None, 'band', 'pw'), may hold values from -6 to 6
- energy_operator_running_sum: bfloat16 [2, 2048, 4, 2048], P(None, None, 'band', 'pw'), may hold values from -6 to 6
- coefficient_store: bfloat16 [4, 512, 2048], P('band'), may hold values from -0.25 to 0.25
- slab_keepers: int32 [2], replicated, may hold values from 0 to 3
- lattice_position: int32 [4, 2048], P('band', 'pw'), may hold values from 0 to 262143
Outputs:
- psi_new: bfloat16 [2, 2048, 4, 2048], P(None, None, 'band', 'pw')
- hpsi_new: bfloat16 [2, 2048, 4, 2048], P(None, None, 'band', 'pw')
The draws below stay inside these ranges and needn't reach their ends.
Inputs may be any that keep to these rules, and one draw needn't show every extreme that they name: `slab_keepers`: each panel's owner is an index along band. `lattice_position`: grid points are row-major indices of a 64 x 64 x 64 grid, not necessarily distinct.
All inputs are finite; a program needn't handle non-finite values.
Results may differ from the reference program's by a relative error of at most 0.001.
Values may be sent and summed in bfloat16 or wider, within the bound.
A program may use at most 128 MiB of HBM per device.

```python
import jax
import jax.numpy as jnp
from jax import lax

RESIDUAL_NUMBER = 512
SLAB_LENGTH = 256
ORBITAL_SPAN = 2048
GRID = 64
PANELS = 2
PWG = 2048
N_BAND = 4


def with_ends(result, own_key, low, high):
    spot = [jax.random.randint(jax.random.fold_in(own_key, axis), (), 0, length) for axis, length in enumerate(result.shape)]
    longest = result.shape.index(max(result.shape))
    beside = spot[:longest] + [(spot[longest] + 1) % result.shape[longest]] + spot[longest + 1:]
    return result.at[tuple(spot)].set(low).at[tuple(beside)].set(high)


def steps_of(key, dims, shards, smallest, top_value):
    gain, own = 1.0, jax.random.fold_in(key, 6)
    for dim, blocks in shards:
        heights = jnp.exp(jax.random.uniform(jax.random.fold_in(own, dim), (blocks,), jnp.float32, smallest / len(shards), top_value / len(shards)))
        gain = gain * jnp.repeat(heights, dims[dim] // blocks).reshape([-1 if axis == dim else 1 for axis in range(len(dims))])
    return gain


def noise(own_key, dims, deviation, bound, shards=(), held_as=jnp.bfloat16):
    level = steps_of(own_key, dims, shards, -0.22, 0.18) if shards else 1.0
    array = jax.random.normal(own_key, dims, jnp.float32) * deviation * level
    return jnp.minimum(jnp.maximum(array, -bound), bound).astype(held_as)


def setup_inputs(seed: int = 0) -> dict:
    streams_of = jax.random.split(jax.random.key(seed), 8)
    return {
        "residual_directions": noise(streams_of[0], (2, RESIDUAL_NUMBER, N_BAND, PWG), 1.0, 6.0, ((1, 8), (2, 4)), jnp.float32),
        "local_field_applied": noise(streams_of[1], (2, RESIDUAL_NUMBER, N_BAND, PWG), 1.0, 6.0, ((1, 8), (2, 4)), jnp.float32),
        "orbital_running_sum": noise(streams_of[2], (2, ORBITAL_SPAN, N_BAND, PWG), 1.0, 6.0, ((2, 4), (3, 8))),
        "energy_operator_running_sum": noise(streams_of[3], (2, ORBITAL_SPAN, N_BAND, PWG), 1.0, 6.0, ((2, 4), (3, 8))),
        "coefficient_store": noise(streams_of[4], (N_BAND, RESIDUAL_NUMBER, ORBITAL_SPAN), RESIDUAL_NUMBER ** -0.5, 0.25, ((0, 4),)),
        "slab_keepers": jax.random.randint(streams_of[5], (PANELS,), 0, N_BAND).astype(jnp.int32),
        "lattice_position": with_ends(jax.random.randint(streams_of[6], (N_BAND, PWG), 0, GRID ** 3), jax.random.fold_in(streams_of[6], 1), 0, (GRID ** 3) - 1).astype(jnp.int32),
    }


def kinetic_of(lattice_position):
    first = lattice_position // (GRID * GRID)
    second = (lattice_position // GRID) % GRID
    third = lattice_position % GRID
    total = jnp.zeros(lattice_position.shape, jnp.int32)
    for index in (first, second, third):
        folded = jnp.where(index >= GRID // 2, index - GRID, index)
        total = total + folded * folded
    return total.astype(jnp.float32) / (GRID * GRID)


def reference(residual_directions, local_field_applied, orbital_running_sum, energy_operator_running_sum, coefficient_store, slab_keepers, lattice_position):
    kinetic = kinetic_of(lattice_position)
    hcorr = kinetic[None, None, :, :] * residual_directions + local_field_applied
    selected_rows = []
    for subspace_slab in range(RESIDUAL_NUMBER // SLAB_LENGTH):
        keeper_processor = slab_keepers[subspace_slab].astype(jnp.int32)
        line_segment = lax.dynamic_index_in_dim(coefficient_store, keeper_processor, 0, keepdims=False)
        selected_rows.append(line_segment[subspace_slab * SLAB_LENGTH:(subspace_slab + 1) * SLAB_LENGTH])
    eigenvector_matrix = jnp.concatenate(selected_rows, axis=0).astype(jnp.float32)

    def one_group(items):
        corr_b, hcorr_b, psi_b, hpsi_b = items
        stacked_vectors = jnp.concatenate([corr_b, hcorr_b], axis=0)
        rotation_product = jnp.einsum("tu,gtm->gum", eigenvector_matrix, stacked_vectors, precision=lax.Precision.HIGHEST)
        psi_out = (psi_b.astype(jnp.float32) + rotation_product[:2]).astype(jnp.bfloat16)
        hpsi_out = (hpsi_b.astype(jnp.float32) + rotation_product[2:]).astype(jnp.bfloat16)
        return psi_out, hpsi_out

    psi_blocks, hpsi_blocks = lax.map(one_group, (jnp.moveaxis(residual_directions, 2, 0), jnp.moveaxis(hcorr, 2, 0), jnp.moveaxis(orbital_running_sum, 2, 0), jnp.moveaxis(energy_operator_running_sum, 2, 0)))
    return jnp.moveaxis(psi_blocks, 0, 2), jnp.moveaxis(hpsi_blocks, 0, 2)
```

```python
import functools

import jax
import jax.numpy as jnp
from jax import lax
from jax.experimental import pallas as pl
from jax.experimental.pallas import tpu as pltpu
from jax.sharding import PartitionSpec as P

GRID = 64
LANES = 128
PARTS = 4
TOP = 32766.0
TILE = 256
MESH = pl.DeviceIdType.MESH


def exchange_kernel(
    n, rows, chunks, keepers_ref, res_ref, loc_ref, store_ref,
    codes_ref, scales_ref, vmat_ref,
    out_codes, out_scales, masked, chip_sum, far_sum,
    code_send, code_recv, scale_send, scale_recv, own_sem,
    sib_send, sib_recv, far_send, far_recv, back_send, back_recv,
):
    me = lax.axis_index("pw")
    band = lax.axis_index("band")
    core = band % 2
    side = band // 2
    sibling = side * 2 + (1 - core)
    across = (1 - side) * 2 + core
    per_dest = chunks // n
    half = store_ref.shape[0] // 2
    part = half // PARTS
    own_start = pl.multiple_of(core * half, half)
    other_start = pl.multiple_of((1 - core) * half, half)

    barrier = pltpu.get_barrier_semaphore()

    def greet(k, _):
        d = (me + 1 + k) % n
        pl.semaphore_signal(barrier, inc=1, device_id={"pw": d}, device_id_type=MESH)
        return 0

    lax.fori_loop(0, n - 1, greet, 0)
    for peer in (sibling, across):
        pl.semaphore_signal(barrier, inc=1, device_id={"band": peer}, device_id_type=MESH)

    for panel in range(2):
        keep = (keepers_ref[panel] == band).astype(jnp.float32).astype(jnp.bfloat16)
        at = pl.ds(panel * half, half)
        masked[at, :] = store_ref[at, :] * keep
    out_scales[...] = jnp.zeros_like(out_scales)

    pl.semaphore_wait(barrier, n + 1)

    def sib_copy(q):
        return pltpu.make_async_remote_copy(
            src_ref=masked.at[pl.ds(other_start + q * part, part)],
            dst_ref=chip_sum.at[pl.ds(q * part, part)],
            send_sem=sib_send.at[q], recv_sem=sib_recv.at[q],
            device_id={"band": sibling}, device_id_type=MESH,
        )

    def far_copy(q):
        return pltpu.make_async_remote_copy(
            src_ref=masked.at[pl.ds(own_start + q * part, part)],
            dst_ref=far_sum.at[pl.ds(q * part, part)],
            send_sem=far_send.at[q], recv_sem=far_recv.at[q],
            device_id={"band": across}, device_id_type=MESH,
        )

    def back_copy(q):
        at = pl.ds(own_start + q * part, part)
        return pltpu.make_async_remote_copy(
            src_ref=vmat_ref.at[at], dst_ref=vmat_ref.at[at],
            send_sem=back_send.at[q], recv_sem=back_recv.at[q],
            device_id={"band": sibling}, device_id_type=MESH,
        )

    def back_arrival(q):
        at = pl.ds(other_start + q * part, part)
        return pltpu.make_async_remote_copy(
            src_ref=vmat_ref.at[at], dst_ref=vmat_ref.at[at],
            send_sem=back_send.at[q], recv_sem=back_recv.at[q],
            device_id={"band": sibling}, device_id_type=MESH,
        )

    for q in range(PARTS):
        sib_copy(q).start()

    def code_copy(k, d):
        return pltpu.make_async_remote_copy(
            src_ref=out_codes.at[d], dst_ref=codes_ref.at[me],
            send_sem=code_send.at[k], recv_sem=code_recv.at[k],
            device_id={"pw": d}, device_id_type=MESH,
        )

    def scale_copy(k, d):
        return pltpu.make_async_remote_copy(
            src_ref=out_scales.at[d], dst_ref=scales_ref.at[me],
            send_sem=scale_send.at[k], recv_sem=scale_recv.at[k],
            device_id={"pw": d}, device_id_type=MESH,
        )

    own_codes = pltpu.make_async_copy(out_codes.at[me], codes_ref.at[me], own_sem.at[0])
    own_scales = pltpu.make_async_copy(out_scales.at[me], scales_ref.at[me], own_sem.at[1])

    def send(k, _):
        d = (me + n // 2 + k) % n
        for a, ref in enumerate((res_ref, loc_ref)):
            for c in range(per_dest):
                lane = pl.ds(c * LANES, LANES)
                both = []
                for plane in range(2):
                    first = plane * rows * chunks + d * per_dest + c
                    x = ref[pl.ds(first, rows, stride=chunks), :]
                    top = jnp.max(jnp.abs(x), axis=0, keepdims=True)
                    inv = jnp.where(top > 1e-30, TOP / jnp.maximum(top, 1e-30), 0.0)
                    both.append(jnp.floor(x * inv + 0.5).astype(jnp.int32))
                    out_scales[d, pl.ds(a * 2 + plane, 1), lane] = top * (1.0 / TOP)
                q = jnp.concatenate(both, axis=0).astype(jnp.int16)
                out_codes[d, pl.ds(a * 2 * rows, 2 * rows), lane] = q

        @pl.when(k != n // 2)
        def _():
            scale_copy(k, d).start()
            code_copy(k, d).start()

        @pl.when(k == n // 2)
        def _():
            own_scales.start()
            own_codes.start()

        return 0

    lax.fori_loop(0, n // 2, send, 0)
    for q in range(PARTS):
        sib_copy(q).wait_recv()
        mine = pl.ds(own_start + q * part, part)
        masked[mine, :] = masked[mine, :] + chip_sum[pl.ds(q * part, part), :]
        far_copy(q).start()
    lax.fori_loop(n // 2, n, send, 0)

    for q in range(PARTS):
        far_copy(q).wait_recv()
        mine = pl.ds(own_start + q * part, part)
        vmat_ref[mine, :] = masked[mine, :] + far_sum[pl.ds(q * part, part), :]
        back_copy(q).start()

    def finish(k, _):
        d = (me + n // 2 + k) % n

        @pl.when(k != n // 2)
        def _():
            scale_copy(k, d).wait()
            code_copy(k, d).wait()

        return 0

    lax.fori_loop(0, n, finish, 0)
    own_scales.wait()
    own_codes.wait()
    for q in range(PARTS):
        sib_copy(q).wait_send()
        far_copy(q).wait_send()
        back_copy(q).wait_send()
        back_arrival(q).wait_recv()


def exchange(n, keepers, res, loc, store):
    planes, rows, _, width = res.shape
    chunks = width // LANES
    span = store.shape[2]
    depth = store.shape[1]
    blocks = 2 * planes * rows
    cols = width // n
    flat = (planes * rows * chunks, LANES)
    dma = pltpu.SemaphoreType.DMA
    vmem = pl.BlockSpec(memory_space=pltpu.VMEM)
    return pl.pallas_call(
        functools.partial(exchange_kernel, n, rows, chunks),
        out_shape=(
            jax.ShapeDtypeStruct((n, blocks, cols), jnp.int16),
            jax.ShapeDtypeStruct((n, 8, cols), jnp.float32),
            jax.ShapeDtypeStruct((depth, span), jnp.bfloat16),
        ),
        in_specs=[pl.BlockSpec(memory_space=pltpu.SMEM), vmem, vmem, vmem],
        out_specs=(
            pl.BlockSpec(memory_space=pl.ANY),
            pl.BlockSpec(memory_space=pl.ANY),
            vmem,
        ),
        scratch_shapes=[
            pltpu.VMEM((n, blocks, cols), jnp.int16),
            pltpu.VMEM((n, 8, cols), jnp.float32),
            pltpu.VMEM((depth, span), jnp.bfloat16),
            pltpu.VMEM((depth // 2, span), jnp.bfloat16),
            pltpu.VMEM((depth // 2, span), jnp.bfloat16),
            dma((n,)), dma((n,)), dma((n,)), dma((n,)), dma((2,)),
            dma((PARTS,)), dma((PARTS,)), dma((PARTS,)), dma((PARTS,)),
            dma((PARTS,)), dma((PARTS,)),
        ],
        compiler_params=pltpu.CompilerParams(
            collective_id=0, has_side_effects=True, vmem_limit_bytes=40 * 2**20
        ),
    )(keepers, res.reshape(flat), loc.reshape(flat), store.reshape(depth, span))


def kinetic_of(lattice_position):
    first = lattice_position // (GRID * GRID)
    second = lattice_position // GRID % GRID
    third = lattice_position % GRID
    total = jnp.zeros(lattice_position.shape, jnp.int32)
    for index in (first, second, third):
        folded = jnp.where(index >= GRID // 2, index - GRID, index)
        total = total + folded * folded
    return total.astype(jnp.float32) / (GRID * GRID)


def rotate_kernel(
    n, rows, codes_ref, scales_ref, kinetic_ref, vmat_ref, psi_ref, hpsi_ref,
    psi_out, hpsi_out, high, low,
):
    cols = codes_ref.shape[2]
    group = max(1, 16 // rows)

    @pl.when(pl.program_id(0) == 0)
    def _():
        kinetic = kinetic_ref[...]

        def columns(s):
            codes = codes_ref[s].astype(jnp.int32).astype(jnp.float32)
            scales = scales_ref[s]
            values = [
                codes[b * rows : (b + 1) * rows] * scales[b : b + 1] for b in range(4)
            ]
            for plane in range(2):
                values[2 + plane] = kinetic * values[plane] + values[2 + plane]
            return jnp.concatenate(values, axis=1)

        def unpack(step, _):
            both = jnp.concatenate(
                [columns(step * group + i) for i in range(group)], axis=0
            )
            top = both.astype(jnp.bfloat16)
            at = pl.ds(pl.multiple_of(step * group * rows, group * rows), group * rows)
            high[at, :] = top
            low[at, :] = (both - top.astype(jnp.float32)).astype(jnp.bfloat16)
            return 0

        lax.fori_loop(0, n // group, unpack, 0)

    dims = (((0,), (0,)), ((), ()))
    v = vmat_ref[...]
    total = lax.dot_general(v, high[...], dims, preferred_element_type=jnp.float32)
    total = total + lax.dot_general(v, low[...], dims, preferred_element_type=jnp.float32)
    for plane in range(2):
        psi = total[:, plane * cols : (plane + 1) * cols]
        hpsi = total[:, (2 + plane) * cols : (3 + plane) * cols]
        psi_out[plane] = (psi_ref[plane].astype(jnp.float32) + psi).astype(jnp.bfloat16)
        hpsi_out[plane] = (hpsi_ref[plane].astype(jnp.float32) + hpsi).astype(jnp.bfloat16)


def rotate(codes, scales, kinetic, vmat, psi, hpsi):
    n, blocks, cols = codes.shape
    rows = blocks // 4
    depth, span = vmat.shape
    whole = lambda shape: pl.BlockSpec(shape, lambda j: (0,) * len(shape))
    band_tile = pl.BlockSpec((2, TILE, cols), lambda j: (0, j, 0))
    out = jax.ShapeDtypeStruct((2, span, cols), jnp.bfloat16)
    return pl.pallas_call(
        functools.partial(rotate_kernel, n, rows),
        grid=(span // TILE,),
        out_shape=(out, out),
        in_specs=[
            whole((n, blocks, cols)),
            whole((n, 8, cols)),
            whole((1, cols)),
            pl.BlockSpec((depth, TILE), lambda j: (0, j)),
            band_tile,
            band_tile,
        ],
        out_specs=(band_tile, band_tile),
        scratch_shapes=[
            pltpu.VMEM((depth, 4 * cols), jnp.bfloat16),
            pltpu.VMEM((depth, 4 * cols), jnp.bfloat16),
        ],
        compiler_params=pltpu.CompilerParams(vmem_limit_bytes=40 * 2**20),
    )(codes, scales, kinetic, vmat, psi, hpsi)


def per_device(n, res, loc, psi, hpsi, store, keepers, lattice):
    codes, scales, vmat = exchange(n, keepers, res, loc, store)
    planes, span, _, cols = psi.shape
    kinetic = kinetic_of(lattice)
    flat = (planes, span, cols)
    psi_new, hpsi_new = rotate(
        codes, scales, kinetic, vmat, psi.reshape(flat), hpsi.reshape(flat)
    )
    return psi_new.reshape(psi.shape), hpsi_new.reshape(hpsi.shape)


def solution(mesh):
    in_specs = (
        P(None, "pw", "band", None),
        P(None, "pw", "band", None),
        P(None, None, "band", "pw"),
        P(None, None, "band", "pw"),
        P("band", None, None),
        P(),
        P("band", "pw"),
    )
    out_specs = (P(None, None, "band", "pw"), P(None, None, "band", "pw"))
    return jax.shard_map(
        functools.partial(per_device, mesh.shape["pw"]),
        mesh=mesh, in_specs=in_specs, out_specs=out_specs, check_vma=False,
    )
```

```python
import functools

import jax
import jax.numpy as jnp
from jax import lax
from jax.experimental import pallas as pl
from jax.experimental.pallas import tpu as pltpu
from jax.sharding import PartitionSpec as P

GRID = 64
LANES = 128
PARTS = 4
TOP = 32766.0
TILE = 256
MESH = pl.DeviceIdType.MESH


def kinetic_of(lattice_position):
    first = lattice_position // (GRID * GRID)
    second = lattice_position // GRID % GRID
    third = lattice_position % GRID
    total = jnp.zeros(lattice_position.shape, jnp.int32)
    for index in (first, second, third):
        folded = jnp.where(index >= GRID // 2, index - GRID, index)
        total = total + folded * folded
    return total.astype(jnp.float32) / (GRID * GRID)


def rotated(v, high, low):
    dims = (((0,), (0,)), ((), ()))
    total = lax.dot_general(v, high, dims, preferred_element_type=jnp.float32)
    return total + lax.dot_general(v, low, dims, preferred_element_type=jnp.float32)


def exchange_kernel(
    n, rows, chunks,
    keepers_hbm, res_hbm, loc_hbm, store_hbm, kinetic_ref, psi_hbm, hpsi_hbm,
    vmat_ref, high1_ref, low1_ref, psi0_ref, hpsi0_ref,
    keepers, res, loc, masked, psi_sum, hpsi_sum,
    out_codes, out_scales, codes, scales, chip_sum, far_sum, high0, low0,
    load_sem, code_send, code_recv, scale_send, scale_recv,
    sib_send, sib_recv, far_send, far_recv, side_send, side_recv, back_send, back_recv,
):
    me = lax.axis_index("pw")
    band = lax.axis_index("band")
    core = band % 2
    side = band // 2
    sibling = side * 2 + (1 - core)
    across = (1 - side) * 2 + core
    parity = me % 2
    beside = me + 1 - 2 * parity
    per_dest = chunks // n
    cols = per_dest * LANES
    half = masked.shape[0] // 2
    part = half // PARTS
    own_start = pl.multiple_of(core * half, half)
    other_start = pl.multiple_of((1 - core) * half, half)

    loads = [
        pltpu.make_async_copy(src, dst, load_sem.at[i])
        for i, (src, dst) in enumerate(
            (
                (keepers_hbm, keepers),
                (res_hbm, res),
                (loc_hbm, loc),
                (store_hbm, masked),
                (psi_hbm.at[0], psi_sum),
                (hpsi_hbm.at[0], hpsi_sum),
            )
        )
    ]
    for load in loads[:4]:
        load.start()

    barrier = pltpu.get_barrier_semaphore()

    def greet(k, _):
        d = (me + 1 + k) % n
        pl.semaphore_signal(barrier, inc=1, device_id={"pw": d}, device_id_type=MESH)
        return 0

    lax.fori_loop(0, n - 1, greet, 0)
    for peer in (sibling, across):
        pl.semaphore_signal(barrier, inc=1, device_id={"band": peer}, device_id_type=MESH)
    out_scales[...] = jnp.zeros_like(out_scales)

    def sib_copy(q):
        return pltpu.make_async_remote_copy(
            src_ref=masked.at[pl.ds(other_start + q * part, part)],
            dst_ref=chip_sum.at[pl.ds(q * part, part)],
            send_sem=sib_send.at[q], recv_sem=sib_recv.at[q],
            device_id={"band": sibling}, device_id_type=MESH,
        )

    def far_copy(i, q):
        return pltpu.make_async_remote_copy(
            src_ref=masked.at[pl.ds(own_start + q * part, part)],
            dst_ref=far_sum.at[pl.ds(q * part, part)],
            send_sem=far_send.at[i], recv_sem=far_recv.at[i],
            device_id={"band": across}, device_id_type=MESH,
        )

    def side_copy(q):
        at = pl.ds(own_start + q * part, part)
        return pltpu.make_async_remote_copy(
            src_ref=vmat_ref.at[at], dst_ref=vmat_ref.at[at],
            send_sem=side_send, recv_sem=side_recv,
            device_id={"pw": beside}, device_id_type=MESH,
        )

    def back_copy(i, start, q):
        at = pl.ds(start + q * part, part)
        return pltpu.make_async_remote_copy(
            src_ref=vmat_ref.at[at], dst_ref=vmat_ref.at[at],
            send_sem=back_send.at[i], recv_sem=back_recv.at[i],
            device_id={"band": sibling}, device_id_type=MESH,
        )

    fetched = (2 + parity, 0, 1, 3 - parity)

    def code_copy(plane, k, d):
        return pltpu.make_async_remote_copy(
            src_ref=out_codes.at[plane, d], dst_ref=codes.at[plane, me],
            send_sem=code_send.at[plane, k], recv_sem=code_recv.at[plane, k],
            device_id={"pw": d}, device_id_type=MESH,
        )

    def scale_copy(plane, k, d):
        return pltpu.make_async_remote_copy(
            src_ref=out_scales.at[plane, d], dst_ref=scales.at[plane, me],
            send_sem=scale_send.at[plane, k], recv_sem=scale_recv.at[plane, k],
            device_id={"pw": d}, device_id_type=MESH,
        )

    def send(plane, k, _):
        d = (me + n // 2 + k) % n
        for c in range(per_dest):
            lane = pl.ds(c * LANES, LANES)
            both, tops = [], []
            for ref in (res, loc):
                first = plane * rows * chunks + d * per_dest + c
                x = ref[pl.ds(first, rows, stride=chunks), :]
                top = jnp.max(jnp.abs(x), axis=0, keepdims=True)
                inv = jnp.where(top > 1e-30, TOP / jnp.maximum(top, 1e-30), 0.0)
                both.append(jnp.floor(x * inv + 0.5).astype(jnp.int32))
                tops.append(top * (1.0 / TOP))
            q = jnp.concatenate(both, axis=0).astype(jnp.int16)

            @pl.when(k != n // 2)
            def _():
                out_codes[plane, d, :, lane] = q
                for a in range(2):
                    out_scales[plane, d, pl.ds(a, 1), lane] = tops[a]

            @pl.when(k == n // 2)
            def _():
                codes[plane, me, :, lane] = q
                for a in range(2):
                    scales[plane, me, pl.ds(a, 1), lane] = tops[a]

        @pl.when(k != n // 2)
        def _():
            scale_copy(plane, k, d).start()
            code_copy(plane, k, d).start()

        return 0

    def arrive(plane, k, _):
        d = (me + n // 2 + k) % n

        @pl.when(k != n // 2)
        def _():
            scale_copy(plane, k, d).wait()
            code_copy(plane, k, d).wait()

        return 0

    def unpack(plane, high, low):
        kinetic = kinetic_of(kinetic_ref[...])
        group = max(1, 16 // rows)

        def columns(s):
            q = codes[plane, s].astype(jnp.int32).astype(jnp.float32)
            scale = scales[plane, s]
            corr = q[:rows] * scale[0:1]
            other = q[rows:] * scale[1:2]
            return jnp.concatenate([corr, kinetic * corr + other], axis=1)

        def step(i, _):
            both = jnp.concatenate([columns(i * group + j) for j in range(group)], axis=0)
            top = both.astype(jnp.bfloat16)
            at = pl.ds(pl.multiple_of(i * group * rows, group * rows), group * rows)
            high[at, :] = top
            low[at, :] = (both - top.astype(jnp.float32)).astype(jnp.bfloat16)
            return 0

        lax.fori_loop(0, n // group, step, 0)

    loads[1].wait()
    loads[2].wait()
    pl.semaphore_wait(barrier, n + 1)
    lax.fori_loop(0, n // 2, functools.partial(send, 0), 0)

    loads[0].wait()
    loads[3].wait()
    for panel in range(2):
        keep = (keepers[panel] == band).astype(jnp.float32).astype(jnp.bfloat16)
        at = pl.ds(panel * half, half)
        masked[at, :] = masked[at, :] * keep
    for q in range(PARTS):
        sib_copy(q).start()
    lax.fori_loop(n // 2, n, functools.partial(send, 0), 0)
    for q in range(PARTS):
        sib_copy(q).wait()
    mine = pl.ds(own_start, half)
    masked[mine, :] = masked[mine, :] + chip_sum[...]
    for i in range(3):
        far_copy(i, fetched[i]).start()
    lax.fori_loop(0, n, functools.partial(send, 1), 0)
    for load in loads[4:]:
        load.start()

    for i in range(3):
        far_copy(i, fetched[i]).wait_recv()
        at = pl.ds(pl.multiple_of(own_start + fetched[i] * part, part), part)
        near = pl.ds(pl.multiple_of(fetched[i] * part, part), part)
        vmat_ref[at, :] = masked[at, :] + far_sum[near, :]
        if i == 0:
            side_copy(fetched[0]).start()
        back_copy(i, own_start, fetched[i]).start()
    side_copy(fetched[0]).wait_send()
    side_copy(fetched[3]).wait_recv()
    back_copy(3, own_start, fetched[3]).start()

    lax.fori_loop(0, n, functools.partial(arrive, 0), 0)
    unpack(0, high0, low0)
    for i in range(PARTS):
        back_copy(i, other_start, fetched[i]).wait_recv()
    for load in loads[4:]:
        load.wait()

    def tile(j, _):
        at = pl.ds(pl.multiple_of(j * TILE, TILE), TILE)
        total = rotated(vmat_ref[:, at], high0[...], low0[...])
        psi0_ref[at, :] = (psi_sum[at, :].astype(jnp.float32) + total[:, :cols]).astype(jnp.bfloat16)
        hpsi0_ref[at, :] = (hpsi_sum[at, :].astype(jnp.float32) + total[:, cols:]).astype(jnp.bfloat16)
        return 0

    lax.fori_loop(0, vmat_ref.shape[1] // TILE, tile, 0)

    lax.fori_loop(0, n, functools.partial(arrive, 1), 0)
    unpack(1, high1_ref, low1_ref)
    for i in range(3):
        far_copy(i, fetched[i]).wait_send()
    for i in range(PARTS):
        back_copy(i, own_start, fetched[i]).wait_send()


def exchange(n, keepers, res, loc, store, lattice, psi, hpsi):
    planes, rows, _, width = res.shape
    chunks = width // LANES
    depth, span = store.shape[1:]
    cols = width // n
    flat = (planes * rows * chunks, LANES)
    dma = pltpu.SemaphoreType.DMA
    vmem = pl.BlockSpec(memory_space=pltpu.VMEM)
    hbm = pl.BlockSpec(memory_space=pltpu.HBM)
    parts = jax.ShapeDtypeStruct((depth, 2 * cols), jnp.bfloat16)
    plane = jax.ShapeDtypeStruct((span, cols), jnp.bfloat16)
    return pl.pallas_call(
        functools.partial(exchange_kernel, n, rows, chunks),
        out_shape=(
            jax.ShapeDtypeStruct((depth, span), jnp.bfloat16), parts, parts, plane, plane,
        ),
        in_specs=[hbm, hbm, hbm, hbm, vmem, hbm, hbm],
        out_specs=(vmem,) * 5,
        scratch_shapes=[
            pltpu.SMEM((2,), jnp.int32),
            pltpu.VMEM(flat, jnp.float32),
            pltpu.VMEM(flat, jnp.float32),
            pltpu.VMEM((depth, span), jnp.bfloat16),
            pltpu.VMEM((span, cols), jnp.bfloat16),
            pltpu.VMEM((span, cols), jnp.bfloat16),
            pltpu.VMEM((planes, n, 2 * rows, cols), jnp.int16),
            pltpu.VMEM((planes, n, 8, cols), jnp.float32),
            pltpu.VMEM((planes, n, 2 * rows, cols), jnp.int16),
            pltpu.VMEM((planes, n, 8, cols), jnp.float32),
            pltpu.VMEM((depth // 2, span), jnp.bfloat16),
            pltpu.VMEM((depth // 2, span), jnp.bfloat16),
            pltpu.VMEM((depth, 2 * cols), jnp.bfloat16),
            pltpu.VMEM((depth, 2 * cols), jnp.bfloat16),
            dma((6,)), dma((planes, n)), dma((planes, n)), dma((planes, n)), dma((planes, n)),
            dma((PARTS,)), dma((PARTS,)), dma((3,)), dma((3,)), dma, dma,
            dma((PARTS,)), dma((PARTS,)),
        ],
        compiler_params=pltpu.CompilerParams(
            collective_id=0, has_side_effects=True, vmem_limit_bytes=50 * 2**20
        ),
    )(
        keepers, res.reshape(flat), loc.reshape(flat), store.reshape(depth, span),
        lattice, psi, hpsi,
    )


def rotate_kernel(
    vmat_ref, high_ref, low_ref, psi0_ref, hpsi0_ref, psi_ref, hpsi_ref, psi_out, hpsi_out
):
    cols = psi0_ref.shape[1]
    total = rotated(vmat_ref[...], high_ref[...], low_ref[...])
    psi_out[0] = psi0_ref[...]
    hpsi_out[0] = hpsi0_ref[...]
    psi_out[1] = (psi_ref[0].astype(jnp.float32) + total[:, :cols]).astype(jnp.bfloat16)
    hpsi_out[1] = (hpsi_ref[0].astype(jnp.float32) + total[:, cols:]).astype(jnp.bfloat16)


def rotate(vmat, high, low, psi0, hpsi0, psi, hpsi):
    depth, span = vmat.shape
    cols = psi0.shape[1]
    halves = pl.BlockSpec((depth, 2 * cols), lambda j: (0, 0))
    done = pl.BlockSpec((TILE, cols), lambda j: (j, 0))
    second = pl.BlockSpec((1, TILE, cols), lambda j: (1, j, 0))
    band_tile = pl.BlockSpec((2, TILE, cols), lambda j: (0, j, 0))
    out = jax.ShapeDtypeStruct((2, span, cols), jnp.bfloat16)
    return pl.pallas_call(
        rotate_kernel,
        grid=(span // TILE,),
        out_shape=(out, out),
        in_specs=[
            pl.BlockSpec((depth, TILE), lambda j: (0, j)),
            halves, halves, done, done, second, second,
        ],
        out_specs=(band_tile, band_tile),
        compiler_params=pltpu.CompilerParams(vmem_limit_bytes=40 * 2**20),
    )(vmat, high, low, psi0, hpsi0, psi, hpsi)


def per_device(n, res, loc, psi, hpsi, store, keepers, lattice):
    planes, span, _, cols = psi.shape
    psi_in, hpsi_in = (x.reshape(planes, span, cols) for x in (psi, hpsi))
    vmat, high, low, psi0, hpsi0 = exchange(
        n, keepers, res, loc, store, lattice, psi_in, hpsi_in
    )
    psi_new, hpsi_new = rotate(vmat, high, low, psi0, hpsi0, psi_in, hpsi_in)
    return psi_new.reshape(psi.shape), hpsi_new.reshape(hpsi.shape)


def solution(mesh):
    in_specs = (
        P(None, "pw", "band", None),
        P(None, "pw", "band", None),
        P(None, None, "band", "pw"),
        P(None, None, "band", "pw"),
        P("band", None, None),
        P(),
        P("band", "pw"),
    )
    out_specs = (P(None, None, "band", "pw"), P(None, None, "band", "pw"))
    return jax.shard_map(
        functools.partial(per_device, mesh.shape["pw"]),
        mesh=mesh, in_specs=in_specs, out_specs=out_specs, check_vma=False,
    )
```

```python
import functools

import jax
import jax.numpy as jnp
from jax import lax
from jax.experimental import pallas as pl
from jax.experimental.pallas import tpu as pltpu
from jax.sharding import PartitionSpec as P

GRID = 64
LANES = 128
PARTS = 4
TOP = 32766.0
TILE = 256
GRANT = 60 * 2**20
MESH = pl.DeviceIdType.MESH


def kinetic_of(lattice_position):
    first = lattice_position // (GRID * GRID)
    second = lattice_position // GRID % GRID
    third = lattice_position % GRID
    total = jnp.zeros(lattice_position.shape, jnp.int32)
    for index in (first, second, third):
        folded = jnp.where(index >= GRID // 2, index - GRID, index)
        total = total + folded * folded
    return total.astype(jnp.float32) / (GRID * GRID)


def rotated(v, high, low):
    dims = (((0,), (0,)), ((), ()))
    total = lax.dot_general(v, high, dims, preferred_element_type=jnp.float32)
    return total + lax.dot_general(v, low, dims, preferred_element_type=jnp.float32)


def exchange_kernel(
    n, rows, chunks,
    keepers_hbm, res_hbm, loc_hbm, store_hbm, lattice_hbm, psi_hbm, hpsi_hbm,
    vmat_out, high_out, low_out, psi0_out, hpsi0_out,
    keepers, res, loc, masked, lattice, psi_sum, hpsi_sum, vmat_ref,
    out_codes, out_scales, codes, scales, chip_sum, far_sum, high0, low0, high1, low1,
    load_sem, store_sem, high_sem, low_sem, code_send, code_recv, scale_send, scale_recv,
    sib_send, sib_recv, far_send, far_recv, side_send, side_recv, back_send, back_recv,
):
    me = lax.axis_index("pw")
    band = lax.axis_index("band")
    core = band % 2
    side = band // 2
    sibling = side * 2 + (1 - core)
    across = (1 - side) * 2 + core
    parity = me % 2
    beside = me + 1 - 2 * parity
    per_dest = chunks // n
    cols = per_dest * LANES
    half = masked.shape[0] // 2
    part = half // PARTS
    own_start = pl.multiple_of(core * half, half)
    other_start = pl.multiple_of((1 - core) * half, half)

    plane_rows = rows * chunks
    loads = [
        pltpu.make_async_copy(src, dst, load_sem.at[i])
        for i, (src, dst) in enumerate(
            (
                (res_hbm.at[pl.ds(0, plane_rows)], res.at[pl.ds(0, plane_rows)]),
                (loc_hbm.at[pl.ds(0, plane_rows)], loc.at[pl.ds(0, plane_rows)]),
                (keepers_hbm, keepers),
                (store_hbm, masked),
                (res_hbm.at[pl.ds(plane_rows, plane_rows)], res.at[pl.ds(plane_rows, plane_rows)]),
                (loc_hbm.at[pl.ds(plane_rows, plane_rows)], loc.at[pl.ds(plane_rows, plane_rows)]),
                (lattice_hbm, lattice),
                (psi_hbm.at[0], psi_sum),
                (hpsi_hbm.at[0], hpsi_sum),
            )
        )
    ]
    for load in loads:
        load.start()

    barrier = pltpu.get_barrier_semaphore()

    def greet(k, _):
        d = (me + 1 + k) % n
        pl.semaphore_signal(barrier, inc=1, device_id={"pw": d}, device_id_type=MESH)
        return 0

    lax.fori_loop(0, n - 1, greet, 0)
    for peer in (sibling, across):
        pl.semaphore_signal(barrier, inc=1, device_id={"band": peer}, device_id_type=MESH)
    out_scales[...] = jnp.zeros_like(out_scales)

    def sib_copy(q):
        return pltpu.make_async_remote_copy(
            src_ref=masked.at[pl.ds(other_start + q * part, part)],
            dst_ref=chip_sum.at[pl.ds(q * part, part)],
            send_sem=sib_send.at[q], recv_sem=sib_recv.at[q],
            device_id={"band": sibling}, device_id_type=MESH,
        )

    def far_copy(i, q):
        return pltpu.make_async_remote_copy(
            src_ref=masked.at[pl.ds(own_start + q * part, part)],
            dst_ref=far_sum.at[pl.ds(q * part, part)],
            send_sem=far_send.at[i], recv_sem=far_recv.at[i],
            device_id={"band": across}, device_id_type=MESH,
        )

    def side_copy(q):
        at = pl.ds(own_start + q * part, part)
        return pltpu.make_async_remote_copy(
            src_ref=vmat_ref.at[at], dst_ref=vmat_ref.at[at],
            send_sem=side_send, recv_sem=side_recv,
            device_id={"pw": beside}, device_id_type=MESH,
        )

    def back_copy(i, start, q):
        at = pl.ds(start + q * part, part)
        return pltpu.make_async_remote_copy(
            src_ref=vmat_ref.at[at], dst_ref=vmat_ref.at[at],
            send_sem=back_send.at[i], recv_sem=back_recv.at[i],
            device_id={"band": sibling}, device_id_type=MESH,
        )

    fetched = (2 + parity, 0, 1, 3 - parity)

    def code_copy(plane, k, d):
        return pltpu.make_async_remote_copy(
            src_ref=out_codes.at[plane, d], dst_ref=codes.at[plane, me],
            send_sem=code_send.at[plane, k], recv_sem=code_recv.at[plane, k],
            device_id={"pw": d}, device_id_type=MESH,
        )

    def scale_copy(plane, k, d):
        return pltpu.make_async_remote_copy(
            src_ref=out_scales.at[plane, d], dst_ref=scales.at[plane, me],
            send_sem=scale_send.at[plane, k], recv_sem=scale_recv.at[plane, k],
            device_id={"pw": d}, device_id_type=MESH,
        )

    def send(plane, k, _):
        d = (me + n // 2 + k) % n
        for c in range(per_dest):
            lane = pl.ds(c * LANES, LANES)
            both, tops = [], []
            for ref in (res, loc):
                first = plane * rows * chunks + d * per_dest + c
                x = ref[pl.ds(first, rows, stride=chunks), :]
                top = jnp.max(jnp.abs(x), axis=0, keepdims=True)
                inv = jnp.where(top > 1e-30, TOP / jnp.maximum(top, 1e-30), 0.0)
                both.append(jnp.floor(x * inv + 0.5).astype(jnp.int32))
                tops.append(top * (1.0 / TOP))
            q = jnp.concatenate(both, axis=0).astype(jnp.int16)

            @pl.when(k != n // 2)
            def _():
                out_codes[plane, d, :, lane] = q
                for a in range(2):
                    out_scales[plane, d, pl.ds(a, 1), lane] = tops[a]

            @pl.when(k == n // 2)
            def _():
                codes[plane, me, :, lane] = q
                for a in range(2):
                    scales[plane, me, pl.ds(a, 1), lane] = tops[a]

        @pl.when(k != n // 2)
        def _():
            scale_copy(plane, k, d).start()
            code_copy(plane, k, d).start()

        return 0

    group = max(1, 16 // rows)

    def rows_copy(i, src, dst, sem):
        at = pl.ds(pl.multiple_of(i * group * rows, group * rows), group * rows)
        return pltpu.make_async_copy(src.at[at], dst.at[at], sem.at[i])

    def receive(plane, high, low):
        kinetic = kinetic_of(lattice[...])

        def arrive(k, _):
            d = (me + n // 2 + k) % n

            @pl.when(k != n // 2)
            def _():
                scale_copy(plane, k, d).wait()
                code_copy(plane, k, d).wait()

            return 0

        def columns(s):
            q = codes[plane, s].astype(jnp.int32).astype(jnp.float32)
            scale = scales[plane, s]
            corr = q[:rows] * scale[0:1]
            other = q[rows:] * scale[1:2]
            return jnp.concatenate([corr, kinetic * corr + other], axis=1)

        def unpack(i):
            both = jnp.concatenate([columns(i * group + j) for j in range(group)], axis=0)
            top = both.astype(jnp.bfloat16)
            at = pl.ds(pl.multiple_of(i * group * rows, group * rows), group * rows)
            high[at, :] = top
            low[at, :] = (both - top.astype(jnp.float32)).astype(jnp.bfloat16)
            if plane == 1:
                rows_copy(i, high, high_out, high_sem).start()
                rows_copy(i, low, low_out, low_sem).start()

        def in_turn(k, _):
            arrive(k, 0)
            unpack((me + 2 * n - n // 2 - k) % n)
            return 0

        def in_order(i, _):
            unpack(i)
            return 0

        if group == 1:
            lax.fori_loop(0, n, in_turn, 0)
        else:
            lax.fori_loop(0, n, arrive, 0)
            lax.fori_loop(0, n // group, in_order, 0)

    loads[0].wait()
    loads[1].wait()
    pl.semaphore_wait(barrier, n + 1)
    lax.fori_loop(0, n // 2, functools.partial(send, 0), 0)

    loads[2].wait()
    loads[3].wait()
    for panel in range(2):
        keep = (keepers[panel] == band).astype(jnp.float32).astype(jnp.bfloat16)
        at = pl.ds(panel * half, half)
        masked[at, :] = masked[at, :] * keep
    for q in range(PARTS):
        sib_copy(q).start()
    lax.fori_loop(n // 2, n, functools.partial(send, 0), 0)
    for q in range(PARTS):
        sib_copy(q).wait()
    mine = pl.ds(own_start, half)
    masked[mine, :] = masked[mine, :] + chip_sum[...]
    for i in range(3):
        far_copy(i, fetched[i]).start()
    loads[4].wait()
    loads[5].wait()
    lax.fori_loop(0, n, functools.partial(send, 1), 0)
    for load in loads[6:]:
        load.wait()

    for i in range(3):
        far_copy(i, fetched[i]).wait_recv()
        at = pl.ds(pl.multiple_of(own_start + fetched[i] * part, part), part)
        near = pl.ds(pl.multiple_of(fetched[i] * part, part), part)
        vmat_ref[at, :] = masked[at, :] + far_sum[near, :]
        if i == 0:
            side_copy(fetched[0]).start()
        back_copy(i, own_start, fetched[i]).start()
    side_copy(fetched[0]).wait_send()
    side_copy(fetched[3]).wait_recv()
    back_copy(3, own_start, fetched[3]).start()

    receive(0, high0, low0)
    for i in range(PARTS):
        back_copy(i, other_start, fetched[i]).wait_recv()
    stores = [
        pltpu.make_async_copy(src, dst, store_sem.at[i])
        for i, (src, dst) in enumerate(
            ((vmat_ref, vmat_out), (psi_sum, psi0_out), (hpsi_sum, hpsi0_out))
        )
    ]
    stores[0].start()

    def tile(j, _):
        at = pl.ds(pl.multiple_of(j * TILE, TILE), TILE)
        total = rotated(vmat_ref[:, at], high0[...], low0[...])
        psi_sum[at, :] = (psi_sum[at, :].astype(jnp.float32) + total[:, :cols]).astype(jnp.bfloat16)
        hpsi_sum[at, :] = (hpsi_sum[at, :].astype(jnp.float32) + total[:, cols:]).astype(jnp.bfloat16)
        return 0

    lax.fori_loop(0, vmat_ref.shape[1] // TILE, tile, 0)
    stores[1].start()
    stores[2].start()

    receive(1, high1, low1)
    for i in range(3):
        far_copy(i, fetched[i]).wait_send()
    for i in range(PARTS):
        back_copy(i, own_start, fetched[i]).wait_send()
    for store in stores:
        store.wait()
    for i in range(n // group):
        rows_copy(i, high1, high_out, high_sem).wait()
        rows_copy(i, low1, low_out, low_sem).wait()


def exchange(n, keepers, res, loc, store, lattice, psi, hpsi):
    planes, rows, _, width = res.shape
    chunks = width // LANES
    depth, span = store.shape[1:]
    cols = width // n
    flat = (planes * rows * chunks, LANES)
    dma = pltpu.SemaphoreType.DMA
    hbm = pl.BlockSpec(memory_space=pltpu.HBM)
    parts = jax.ShapeDtypeStruct((depth, 2 * cols), jnp.bfloat16)
    plane = jax.ShapeDtypeStruct((span, cols), jnp.bfloat16)
    return pl.pallas_call(
        functools.partial(exchange_kernel, n, rows, chunks),
        out_shape=(
            jax.ShapeDtypeStruct((depth, span), jnp.bfloat16), parts, parts, plane, plane,
        ),
        in_specs=[hbm] * 7,
        out_specs=(hbm,) * 5,
        scratch_shapes=[
            pltpu.SMEM((2,), jnp.int32),
            pltpu.VMEM(flat, jnp.float32),
            pltpu.VMEM(flat, jnp.float32),
            pltpu.VMEM((depth, span), jnp.bfloat16),
            pltpu.VMEM(lattice.shape, jnp.int32),
            pltpu.VMEM((span, cols), jnp.bfloat16),
            pltpu.VMEM((span, cols), jnp.bfloat16),
            pltpu.VMEM((depth, span), jnp.bfloat16),
            pltpu.VMEM((planes, n, 2 * rows, cols), jnp.int16),
            pltpu.VMEM((planes, n, 8, cols), jnp.float32),
            pltpu.VMEM((planes, n, 2 * rows, cols), jnp.int16),
            pltpu.VMEM((planes, n, 8, cols), jnp.float32),
            pltpu.VMEM((depth // 2, span), jnp.bfloat16),
            pltpu.VMEM((depth // 2, span), jnp.bfloat16),
            pltpu.VMEM((depth, 2 * cols), jnp.bfloat16),
            pltpu.VMEM((depth, 2 * cols), jnp.bfloat16),
            pltpu.VMEM((depth, 2 * cols), jnp.bfloat16),
            pltpu.VMEM((depth, 2 * cols), jnp.bfloat16),
            dma((9,)), dma((3,)), dma((n,)), dma((n,)), dma((planes, n)), dma((planes, n)), dma((planes, n)), dma((planes, n)),
            dma((PARTS,)), dma((PARTS,)), dma((3,)), dma((3,)), dma, dma,
            dma((PARTS,)), dma((PARTS,)),
        ],
        compiler_params=pltpu.CompilerParams(
            collective_id=0, has_side_effects=True, vmem_limit_bytes=GRANT
        ),
    )(
        keepers, res.reshape(flat), loc.reshape(flat), store.reshape(depth, span),
        lattice, psi, hpsi,
    )


def rotate_kernel(
    vmat_hbm, high_hbm, low_hbm, psi0_hbm, hpsi0_hbm, psi_hbm, hpsi_hbm,
    psi_out, hpsi_out,
    vmat, high, low, psi, hpsi, load_sem, vmat_sem, plane_sem, psi_sem, hpsi_sem,
):
    span, cols = psi.shape
    tiles = span // TILE

    def tile(j):
        return pl.ds(pl.multiple_of(j * TILE, TILE), TILE)

    def vmat_copy(j):
        return pltpu.make_async_copy(
            vmat_hbm.at[:, tile(j)], vmat.at[:, tile(j)], vmat_sem.at[j]
        )

    def out_copy(j, src, dst, sem):
        return pltpu.make_async_copy(src.at[tile(j)], dst.at[1, tile(j)], sem.at[j])

    loads = [
        pltpu.make_async_copy(src, dst, load_sem.at[i])
        for i, (src, dst) in enumerate(
            ((high_hbm, high), (low_hbm, low), (psi_hbm.at[1], psi), (hpsi_hbm.at[1], hpsi))
        )
    ]
    first = [
        pltpu.make_async_copy(psi0_hbm, psi_out.at[0], plane_sem.at[0]),
        pltpu.make_async_copy(hpsi0_hbm, hpsi_out.at[0], plane_sem.at[1]),
    ]
    loads[0].start()
    loads[1].start()
    vmat_copy(0).start()
    loads[2].start()
    loads[3].start()
    for j in range(1, tiles):
        vmat_copy(j).start()
    for copy in first:
        copy.start()
    for load in loads:
        load.wait()

    def step(j, _):
        vmat_copy(j).wait()
        at = tile(j)
        total = rotated(vmat[:, at], high[...], low[...])
        psi[at, :] = (psi[at, :].astype(jnp.float32) + total[:, :cols]).astype(jnp.bfloat16)
        hpsi[at, :] = (hpsi[at, :].astype(jnp.float32) + total[:, cols:]).astype(jnp.bfloat16)
        out_copy(j, psi, psi_out, psi_sem).start()
        out_copy(j, hpsi, hpsi_out, hpsi_sem).start()
        return 0

    lax.fori_loop(0, tiles, step, 0)
    for j in range(tiles):
        out_copy(j, psi, psi_out, psi_sem).wait()
        out_copy(j, hpsi, hpsi_out, hpsi_sem).wait()
    for copy in first:
        copy.wait()


def rotate(vmat, high, low, psi0, hpsi0, psi, hpsi):
    depth, span = vmat.shape
    cols = psi0.shape[1]
    tiles = span // TILE
    dma = pltpu.SemaphoreType.DMA
    hbm = pl.BlockSpec(memory_space=pltpu.HBM)
    out = jax.ShapeDtypeStruct((2, span, cols), jnp.bfloat16)
    return pl.pallas_call(
        rotate_kernel,
        out_shape=(out, out),
        in_specs=[hbm] * 7,
        out_specs=(hbm, hbm),
        scratch_shapes=[
            pltpu.VMEM((depth, span), jnp.bfloat16),
            pltpu.VMEM((depth, 2 * cols), jnp.bfloat16),
            pltpu.VMEM((depth, 2 * cols), jnp.bfloat16),
            pltpu.VMEM((span, cols), jnp.bfloat16),
            pltpu.VMEM((span, cols), jnp.bfloat16),
            dma((4,)), dma((tiles,)), dma((2,)), dma((tiles,)), dma((tiles,)),
        ],
        compiler_params=pltpu.CompilerParams(vmem_limit_bytes=GRANT),
    )(vmat, high, low, psi0, hpsi0, psi, hpsi)


def per_device(n, res, loc, psi, hpsi, store, keepers, lattice):
    planes, span, _, cols = psi.shape
    psi_in, hpsi_in = (x.reshape(planes, span, cols) for x in (psi, hpsi))
    vmat, high, low, psi0, hpsi0 = exchange(
        n, keepers, res, loc, store, lattice, psi_in, hpsi_in
    )
    psi_new, hpsi_new = rotate(vmat, high, low, psi0, hpsi0, psi_in, hpsi_in)
    return psi_new.reshape(psi.shape), hpsi_new.reshape(hpsi.shape)


def solution(mesh):
    in_specs = (
        P(None, "pw", "band", None),
        P(None, "pw", "band", None),
        P(None, None, "band", "pw"),
        P(None, None, "band", "pw"),
        P("band", None, None),
        P(),
        P("band", "pw"),
    )
    out_specs = (P(None, None, "band", "pw"), P(None, None, "band", "pw"))
    return jax.shard_map(
        functools.partial(per_device, mesh.shape["pw"]),
        mesh=mesh, in_specs=in_specs, out_specs=out_specs, check_vma=False,
    )
```

```python
import functools

import jax
import jax.numpy as jnp
from jax import lax
from jax.experimental import pallas as pl
from jax.experimental.pallas import tpu as pltpu
from jax.sharding import PartitionSpec as P

GRID = 64
LANES = 128
PARTS = 4
TOP = 32766.0
TILE = 256
GRANT = 60 * 2**20
MESH = pl.DeviceIdType.MESH


def kinetic_of(lattice_position):
    first = lattice_position // (GRID * GRID)
    second = lattice_position // GRID % GRID
    third = lattice_position % GRID
    total = jnp.zeros(lattice_position.shape, jnp.int32)
    for index in (first, second, third):
        folded = jnp.where(index >= GRID // 2, index - GRID, index)
        total = total + folded * folded
    return total.astype(jnp.float32) / (GRID * GRID)


def rotated(v, high, low):
    dims = (((0,), (0,)), ((), ()))
    total = lax.dot_general(v, high, dims, preferred_element_type=jnp.float32)
    return total + lax.dot_general(v, low, dims, preferred_element_type=jnp.float32)


def exchange_kernel(
    n, rows, chunks,
    keepers_hbm, res_hbm, loc_hbm, store_hbm, lattice_hbm, psi_hbm, hpsi_hbm,
    vmat_out, high_out, low_out, psi0_out, hpsi0_out,
    keepers, res, loc, masked, lattice, psi_sum, hpsi_sum, vmat_ref,
    out_codes, out_scales, codes, scales, chip_sum, far_sum, high0, low0, high1, low1,
    load_sem, store_sem, high_sem, low_sem, code_send, code_recv, scale_send, scale_recv,
    sib_send, sib_recv, far_send, far_recv, side_send, side_recv, back_send, back_recv,
):
    me = lax.axis_index("pw")
    band = lax.axis_index("band")
    core = band % 2
    side = band // 2
    sibling = side * 2 + (1 - core)
    across = (1 - side) * 2 + core
    parity = me % 2
    beside = me + 1 - 2 * parity
    per_dest = chunks // n
    cols = per_dest * LANES
    half = masked.shape[0] // 2
    part = half // PARTS
    own_start = pl.multiple_of(core * half, half)
    other_start = pl.multiple_of((1 - core) * half, half)

    plane_rows = rows * chunks
    first, second = pl.ds(0, plane_rows), pl.ds(plane_rows, plane_rows)
    other, mine = pl.ds(other_start, half), pl.ds(own_start, half)
    loads = [
        pltpu.make_async_copy(src, dst, load_sem.at[i])
        for i, (src, dst) in enumerate(
            (
                (keepers_hbm, keepers),
                (store_hbm.at[other], masked.at[other]),
                (res_hbm.at[first], res.at[first]),
                (loc_hbm.at[first], loc.at[first]),
                (store_hbm.at[mine], masked.at[mine]),
                (res_hbm.at[second], res.at[second]),
                (loc_hbm.at[second], loc.at[second]),
                (lattice_hbm, lattice),
                (psi_hbm.at[0], psi_sum),
                (hpsi_hbm.at[0], hpsi_sum),
            )
        )
    ]
    for load in loads:
        load.start()

    barrier = pltpu.get_barrier_semaphore()

    def greet(k, _):
        d = (me + 1 + k) % n
        pl.semaphore_signal(barrier, inc=1, device_id={"pw": d}, device_id_type=MESH)
        return 0

    lax.fori_loop(0, n - 1, greet, 0)
    for peer in (sibling, across):
        pl.semaphore_signal(barrier, inc=1, device_id={"band": peer}, device_id_type=MESH)
    out_scales[...] = jnp.zeros_like(out_scales)

    def sib_copy(i, q):
        return pltpu.make_async_remote_copy(
            src_ref=masked.at[pl.ds(other_start + q * part, part)],
            dst_ref=chip_sum.at[pl.ds(q * part, part)],
            send_sem=sib_send.at[i], recv_sem=sib_recv.at[i],
            device_id={"band": sibling}, device_id_type=MESH,
        )

    def far_copy(i, q):
        return pltpu.make_async_remote_copy(
            src_ref=masked.at[pl.ds(own_start + q * part, part)],
            dst_ref=far_sum.at[pl.ds(q * part, part)],
            send_sem=far_send.at[i], recv_sem=far_recv.at[i],
            device_id={"band": across}, device_id_type=MESH,
        )

    def side_copy(q):
        at = pl.ds(own_start + q * part, part)
        return pltpu.make_async_remote_copy(
            src_ref=vmat_ref.at[at], dst_ref=vmat_ref.at[at],
            send_sem=side_send, recv_sem=side_recv,
            device_id={"pw": beside}, device_id_type=MESH,
        )

    def back_copy(i, start, q):
        at = pl.ds(start + q * part, part)
        return pltpu.make_async_remote_copy(
            src_ref=vmat_ref.at[at], dst_ref=vmat_ref.at[at],
            send_sem=back_send.at[i], recv_sem=back_recv.at[i],
            device_id={"band": sibling}, device_id_type=MESH,
        )

    fetched = (2 + parity, 0, 1, 3 - parity)

    def code_copy(plane, k, d):
        return pltpu.make_async_remote_copy(
            src_ref=out_codes.at[plane, d], dst_ref=codes.at[plane, me],
            send_sem=code_send.at[plane, k], recv_sem=code_recv.at[plane, k],
            device_id={"pw": d}, device_id_type=MESH,
        )

    def scale_copy(plane, k, d):
        return pltpu.make_async_remote_copy(
            src_ref=out_scales.at[plane, d], dst_ref=scales.at[plane, me],
            send_sem=scale_send.at[plane, k], recv_sem=scale_recv.at[plane, k],
            device_id={"pw": d}, device_id_type=MESH,
        )

    def send(plane, k, _):
        d = (me + n // 2 + k) % n
        for c in range(per_dest):
            lane = pl.ds(c * LANES, LANES)
            both, tops = [], []
            for ref in (res, loc):
                first = plane * rows * chunks + d * per_dest + c
                x = ref[pl.ds(first, rows, stride=chunks), :]
                top = jnp.max(jnp.abs(x), axis=0, keepdims=True)
                inv = jnp.where(top > 1e-30, TOP / jnp.maximum(top, 1e-30), 0.0)
                both.append(jnp.floor(x * inv + 0.5).astype(jnp.int32))
                tops.append(top * (1.0 / TOP))
            q = jnp.concatenate(both, axis=0).astype(jnp.int16)

            @pl.when(k != n // 2)
            def _():
                out_codes[plane, d, :, lane] = q
                for a in range(2):
                    out_scales[plane, d, pl.ds(a, 1), lane] = tops[a]

            @pl.when(k == n // 2)
            def _():
                codes[plane, me, :, lane] = q
                for a in range(2):
                    scales[plane, me, pl.ds(a, 1), lane] = tops[a]

        @pl.when(k != n // 2)
        def _():
            scale_copy(plane, k, d).start()
            code_copy(plane, k, d).start()

        return 0

    group = max(1, 16 // rows)

    def rows_copy(i, src, dst, sem):
        at = pl.ds(pl.multiple_of(i * group * rows, group * rows), group * rows)
        return pltpu.make_async_copy(src.at[at], dst.at[at], sem.at[i])

    def receive(plane, high, low):
        kinetic = kinetic_of(lattice[...])

        def arrive(k, _):
            d = (me + n // 2 + k) % n

            @pl.when(k != n // 2)
            def _():
                scale_copy(plane, k, d).wait()
                code_copy(plane, k, d).wait()

            return 0

        def columns(s):
            q = codes[plane, s].astype(jnp.int32).astype(jnp.float32)
            scale = scales[plane, s]
            corr = q[:rows] * scale[0:1]
            other = q[rows:] * scale[1:2]
            return jnp.concatenate([corr, kinetic * corr + other], axis=1)

        def unpack(i):
            both = jnp.concatenate([columns(i * group + j) for j in range(group)], axis=0)
            top = both.astype(jnp.bfloat16)
            at = pl.ds(pl.multiple_of(i * group * rows, group * rows), group * rows)
            high[at, :] = top
            low[at, :] = (both - top.astype(jnp.float32)).astype(jnp.bfloat16)
            if plane == 1:
                rows_copy(i, high, high_out, high_sem).start()
                rows_copy(i, low, low_out, low_sem).start()

        def in_turn(k, _):
            arrive(k, 0)
            unpack((me + 2 * n - n // 2 - k) % n)
            return 0

        def in_order(i, _):
            unpack(i)
            return 0

        if group == 1:
            lax.fori_loop(0, n, in_turn, 0)
        else:
            lax.fori_loop(0, n, arrive, 0)
            lax.fori_loop(0, n // group, in_order, 0)

    def keep(panel):
        return (keepers[panel] == band).astype(jnp.float32).astype(jnp.bfloat16)

    loads[0].wait()
    loads[1].wait()
    pl.semaphore_wait(barrier, n + 1)
    for i in range(3):
        at = pl.ds(pl.multiple_of(other_start + fetched[i] * part, part), part)
        masked[at, :] = masked[at, :] * keep(1 - core)
        sib_copy(i, fetched[i]).start()
    loads[2].wait()
    loads[3].wait()
    lax.fori_loop(0, n // 2, functools.partial(send, 0), 0)
    loads[4].wait()
    for i in range(3):
        sib_copy(i, fetched[i]).wait_recv()
        at = pl.ds(pl.multiple_of(own_start + fetched[i] * part, part), part)
        near = pl.ds(pl.multiple_of(fetched[i] * part, part), part)
        masked[at, :] = masked[at, :] * keep(core) + chip_sum[near, :]
        far_copy(i, fetched[i]).start()
    lax.fori_loop(n // 2, n, functools.partial(send, 0), 0)
    loads[5].wait()
    loads[6].wait()
    lax.fori_loop(0, n, functools.partial(send, 1), 0)
    for load in loads[7:]:
        load.wait()

    for i in range(3):
        far_copy(i, fetched[i]).wait_recv()
        at = pl.ds(pl.multiple_of(own_start + fetched[i] * part, part), part)
        near = pl.ds(pl.multiple_of(fetched[i] * part, part), part)
        vmat_ref[at, :] = masked[at, :] + far_sum[near, :]
        if i == 0:
            side_copy(fetched[0]).start()
        back_copy(i, own_start, fetched[i]).start()
    side_copy(fetched[0]).wait_send()
    side_copy(fetched[3]).wait_recv()
    back_copy(3, own_start, fetched[3]).start()

    receive(0, high0, low0)
    for i in range(PARTS):
        back_copy(i, other_start, fetched[i]).wait_recv()
    stores = [
        pltpu.make_async_copy(src, dst, store_sem.at[i])
        for i, (src, dst) in enumerate(
            ((vmat_ref, vmat_out), (psi_sum, psi0_out), (hpsi_sum, hpsi0_out))
        )
    ]
    stores[0].start()

    def tile(j, _):
        at = pl.ds(pl.multiple_of(j * TILE, TILE), TILE)
        total = rotated(vmat_ref[:, at], high0[...], low0[...])
        psi_sum[at, :] = (psi_sum[at, :].astype(jnp.float32) + total[:, :cols]).astype(jnp.bfloat16)
        hpsi_sum[at, :] = (hpsi_sum[at, :].astype(jnp.float32) + total[:, cols:]).astype(jnp.bfloat16)
        return 0

    lax.fori_loop(0, vmat_ref.shape[1] // TILE, tile, 0)
    stores[1].start()
    stores[2].start()

    receive(1, high1, low1)
    for i in range(3):
        sib_copy(i, fetched[i]).wait_send()
        far_copy(i, fetched[i]).wait_send()
    for i in range(PARTS):
        back_copy(i, own_start, fetched[i]).wait_send()
    for store in stores:
        store.wait()
    for i in range(n // group):
        rows_copy(i, high1, high_out, high_sem).wait()
        rows_copy(i, low1, low_out, low_sem).wait()


def exchange(n, keepers, res, loc, store, lattice, psi, hpsi):
    planes, rows, _, width = res.shape
    chunks = width // LANES
    depth, span = store.shape[1:]
    cols = width // n
    flat = (planes * rows * chunks, LANES)
    dma = pltpu.SemaphoreType.DMA
    hbm = pl.BlockSpec(memory_space=pltpu.HBM)
    parts = jax.ShapeDtypeStruct((depth, 2 * cols), jnp.bfloat16)
    plane = jax.ShapeDtypeStruct((span, cols), jnp.bfloat16)
    return pl.pallas_call(
        functools.partial(exchange_kernel, n, rows, chunks),
        out_shape=(
            jax.ShapeDtypeStruct((depth, span), jnp.bfloat16), parts, parts, plane, plane,
        ),
        in_specs=[hbm] * 7,
        out_specs=(hbm,) * 5,
        scratch_shapes=[
            pltpu.SMEM((2,), jnp.int32),
            pltpu.VMEM(flat, jnp.float32),
            pltpu.VMEM(flat, jnp.float32),
            pltpu.VMEM((depth, span), jnp.bfloat16),
            pltpu.VMEM(lattice.shape, jnp.int32),
            pltpu.VMEM((span, cols), jnp.bfloat16),
            pltpu.VMEM((span, cols), jnp.bfloat16),
            pltpu.VMEM((depth, span), jnp.bfloat16),
            pltpu.VMEM((planes, n, 2 * rows, cols), jnp.int16),
            pltpu.VMEM((planes, n, 8, cols), jnp.float32),
            pltpu.VMEM((planes, n, 2 * rows, cols), jnp.int16),
            pltpu.VMEM((planes, n, 8, cols), jnp.float32),
            pltpu.VMEM((depth // 2, span), jnp.bfloat16),
            pltpu.VMEM((depth // 2, span), jnp.bfloat16),
            pltpu.VMEM((depth, 2 * cols), jnp.bfloat16),
            pltpu.VMEM((depth, 2 * cols), jnp.bfloat16),
            pltpu.VMEM((depth, 2 * cols), jnp.bfloat16),
            pltpu.VMEM((depth, 2 * cols), jnp.bfloat16),
            dma((10,)), dma((3,)), dma((n,)), dma((n,)), dma((planes, n)), dma((planes, n)), dma((planes, n)), dma((planes, n)),
            dma((3,)), dma((3,)), dma((3,)), dma((3,)), dma, dma,
            dma((PARTS,)), dma((PARTS,)),
        ],
        compiler_params=pltpu.CompilerParams(
            collective_id=0, has_side_effects=True, vmem_limit_bytes=GRANT
        ),
    )(
        keepers, res.reshape(flat), loc.reshape(flat), store.reshape(depth, span),
        lattice, psi, hpsi,
    )


def rotate_kernel(
    vmat_hbm, high_hbm, low_hbm, psi0_hbm, hpsi0_hbm, psi_hbm, hpsi_hbm,
    psi_out, hpsi_out,
    vmat, high, low, psi, hpsi, psi0, hpsi0,
    load_sem, vmat_sem, plane_sem, psi_sem, hpsi_sem,
):
    span, cols = psi.shape
    tiles = span // TILE

    def tile(j):
        return pl.ds(pl.multiple_of(j * TILE, TILE), TILE)

    def vmat_copy(j):
        return pltpu.make_async_copy(
            vmat_hbm.at[:, tile(j)], vmat.at[:, tile(j)], vmat_sem.at[j]
        )

    def out_copy(j, src, dst, sem):
        return pltpu.make_async_copy(src.at[tile(j)], dst.at[1, tile(j)], sem.at[j])

    loads = [
        pltpu.make_async_copy(src, dst, load_sem.at[i])
        for i, (src, dst) in enumerate(
            (
                (high_hbm, high),
                (low_hbm, low),
                (psi_hbm.at[1], psi),
                (hpsi_hbm.at[1], hpsi),
                (psi0_hbm, psi0),
                (hpsi0_hbm, hpsi0),
            )
        )
    ]
    first = [
        pltpu.make_async_copy(psi0, psi_out.at[0], plane_sem.at[0]),
        pltpu.make_async_copy(hpsi0, hpsi_out.at[0], plane_sem.at[1]),
    ]
    loads[0].start()
    loads[1].start()
    vmat_copy(0).start()
    loads[2].start()
    loads[3].start()
    for j in range(1, tiles):
        vmat_copy(j).start()
    loads[4].start()
    loads[5].start()
    for load in loads[:4]:
        load.wait()

    def step(j, _):
        vmat_copy(j).wait()
        at = tile(j)
        total = rotated(vmat[:, at], high[...], low[...])
        psi[at, :] = (psi[at, :].astype(jnp.float32) + total[:, :cols]).astype(jnp.bfloat16)
        hpsi[at, :] = (hpsi[at, :].astype(jnp.float32) + total[:, cols:]).astype(jnp.bfloat16)
        out_copy(j, psi, psi_out, psi_sem).start()
        out_copy(j, hpsi, hpsi_out, hpsi_sem).start()
        return 0

    lax.fori_loop(0, tiles // 2, step, 0)
    for i in range(2):
        loads[4 + i].wait()
        first[i].start()
    lax.fori_loop(tiles // 2, tiles, step, 0)
    for j in range(tiles):
        out_copy(j, psi, psi_out, psi_sem).wait()
        out_copy(j, hpsi, hpsi_out, hpsi_sem).wait()
    for copy in first:
        copy.wait()


def rotate(vmat, high, low, psi0, hpsi0, psi, hpsi):
    depth, span = vmat.shape
    cols = psi0.shape[1]
    tiles = span // TILE
    dma = pltpu.SemaphoreType.DMA
    hbm = pl.BlockSpec(memory_space=pltpu.HBM)
    out = jax.ShapeDtypeStruct((2, span, cols), jnp.bfloat16)
    return pl.pallas_call(
        rotate_kernel,
        out_shape=(out, out),
        in_specs=[hbm] * 7,
        out_specs=(hbm, hbm),
        scratch_shapes=[
            pltpu.VMEM((depth, span), jnp.bfloat16),
            pltpu.VMEM((depth, 2 * cols), jnp.bfloat16),
            pltpu.VMEM((depth, 2 * cols), jnp.bfloat16),
            pltpu.VMEM((span, cols), jnp.bfloat16),
            pltpu.VMEM((span, cols), jnp.bfloat16),
            pltpu.VMEM((span, cols), jnp.bfloat16),
            pltpu.VMEM((span, cols), jnp.bfloat16),
            dma((6,)), dma((tiles,)), dma((2,)), dma((tiles,)), dma((tiles,)),
        ],
        compiler_params=pltpu.CompilerParams(vmem_limit_bytes=GRANT),
    )(vmat, high, low, psi0, hpsi0, psi, hpsi)


def per_device(n, res, loc, psi, hpsi, store, keepers, lattice):
    planes, span, _, cols = psi.shape
    psi_in, hpsi_in = (x.reshape(planes, span, cols) for x in (psi, hpsi))
    vmat, high, low, psi0, hpsi0 = exchange(
        n, keepers, res, loc, store, lattice, psi_in, hpsi_in
    )
    psi_new, hpsi_new = rotate(vmat, high, low, psi0, hpsi0, psi_in, hpsi_in)
    return psi_new.reshape(psi.shape), hpsi_new.reshape(hpsi.shape)


def solution(mesh):
    in_specs = (
        P(None, "pw", "band", None),
        P(None, "pw", "band", None),
        P(None, None, "band", "pw"),
        P(None, None, "band", "pw"),
        P("band", None, None),
        P(),
        P("band", "pw"),
    )
    out_specs = (P(None, None, "band", "pw"), P(None, None, "band", "pw"))
    return jax.shard_map(
        functools.partial(per_device, mesh.shape["pw"]),
        mesh=mesh, in_specs=in_specs, out_specs=out_specs, check_vma=False,
    )
```

```python
import functools

import jax
import jax.numpy as jnp
from jax import lax
from jax.experimental import pallas as pl
from jax.experimental.pallas import tpu as pltpu
from jax.sharding import PartitionSpec as P

GRID = 64
LANES = 128
PARTS = 4
TOP = 32766.0
TILE = 512
GRANT = 60 * 2**20
MESH = pl.DeviceIdType.MESH


def kinetic_of(lattice_position):
    first = lattice_position // (GRID * GRID)
    second = lattice_position // GRID % GRID
    third = lattice_position % GRID
    total = jnp.zeros(lattice_position.shape, jnp.int32)
    for index in (first, second, third):
        folded = jnp.where(index >= GRID // 2, index - GRID, index)
        total = total + folded * folded
    return total.astype(jnp.float32) / (GRID * GRID)


def rotated(v, pieces):
    dims = (((0,), (0,)), ((), ()))
    total = lax.dot_general(v, pieces, dims, preferred_element_type=jnp.float32)
    width = total.shape[1] // 2
    return total[:, :width] + total[:, width:]


def exchange_kernel(
    n, rows, chunks,
    keepers_hbm, res_hbm, loc_hbm, store_hbm, lattice_hbm, psi_hbm, hpsi_hbm,
    vmat_out, pieces_out, psi0_out, hpsi0_out,
    keepers, res, loc, masked, lattice, psi_sum, hpsi_sum, vmat_ref,
    out_codes, out_scales, codes, scales, chip_sum, far_sum, pieces0, pieces1,
    load_sem, store_sem, pieces_sem, code_send, code_recv, scale_send, scale_recv,
    sib_send, sib_recv, far_send, far_recv, side_send, side_recv, back_send, back_recv,
):
    me = lax.axis_index("pw")
    band = lax.axis_index("band")
    core = band % 2
    side = band // 2
    sibling = side * 2 + (1 - core)
    across = (1 - side) * 2 + core
    parity = me % 2
    beside = me + 1 - 2 * parity
    per_dest = chunks // n
    cols = per_dest * LANES
    half = masked.shape[0] // 2
    part = half // PARTS
    own_start = pl.multiple_of(core * half, half)
    other_start = pl.multiple_of((1 - core) * half, half)

    plane_rows = rows * chunks
    first, second = pl.ds(0, plane_rows), pl.ds(plane_rows, plane_rows)
    other, mine = pl.ds(other_start, half), pl.ds(own_start, half)
    loads = [
        pltpu.make_async_copy(src, dst, load_sem.at[i])
        for i, (src, dst) in enumerate(
            (
                (keepers_hbm, keepers),
                (store_hbm.at[other], masked.at[other]),
                (res_hbm.at[first], res.at[first]),
                (loc_hbm.at[first], loc.at[first]),
                (store_hbm.at[mine], masked.at[mine]),
                (res_hbm.at[second], res.at[second]),
                (loc_hbm.at[second], loc.at[second]),
                (lattice_hbm, lattice),
                (psi_hbm.at[0], psi_sum),
                (hpsi_hbm.at[0], hpsi_sum),
            )
        )
    ]
    for load in loads:
        load.start()

    barrier = pltpu.get_barrier_semaphore()

    def greet(k, _):
        d = (me + 1 + k) % n
        pl.semaphore_signal(barrier, inc=1, device_id={"pw": d}, device_id_type=MESH)
        return 0

    lax.fori_loop(0, n - 1, greet, 0)
    for peer in (sibling, across):
        pl.semaphore_signal(barrier, inc=1, device_id={"band": peer}, device_id_type=MESH)
    out_scales[...] = jnp.zeros_like(out_scales)

    def sib_copy(i, q):
        return pltpu.make_async_remote_copy(
            src_ref=masked.at[pl.ds(other_start + q * part, part)],
            dst_ref=chip_sum.at[pl.ds(q * part, part)],
            send_sem=sib_send.at[i], recv_sem=sib_recv.at[i],
            device_id={"band": sibling}, device_id_type=MESH,
        )

    def far_copy(i, q):
        return pltpu.make_async_remote_copy(
            src_ref=masked.at[pl.ds(own_start + q * part, part)],
            dst_ref=far_sum.at[pl.ds(q * part, part)],
            send_sem=far_send.at[i], recv_sem=far_recv.at[i],
            device_id={"band": across}, device_id_type=MESH,
        )

    def side_copy(q):
        at = pl.ds(own_start + q * part, part)
        return pltpu.make_async_remote_copy(
            src_ref=vmat_ref.at[at], dst_ref=vmat_ref.at[at],
            send_sem=side_send, recv_sem=side_recv,
            device_id={"pw": beside}, device_id_type=MESH,
        )

    def back_copy(i, start, q):
        at = pl.ds(start + q * part, part)
        return pltpu.make_async_remote_copy(
            src_ref=vmat_ref.at[at], dst_ref=vmat_ref.at[at],
            send_sem=back_send.at[i], recv_sem=back_recv.at[i],
            device_id={"band": sibling}, device_id_type=MESH,
        )

    fetched = (2 + parity, 0, 1, 3 - parity)

    def code_copy(plane, k, d):
        return pltpu.make_async_remote_copy(
            src_ref=out_codes.at[plane, d], dst_ref=codes.at[plane, me],
            send_sem=code_send.at[plane, k], recv_sem=code_recv.at[plane, k],
            device_id={"pw": d}, device_id_type=MESH,
        )

    def scale_copy(plane, k, d):
        return pltpu.make_async_remote_copy(
            src_ref=out_scales.at[plane, d], dst_ref=scales.at[plane, me],
            send_sem=scale_send.at[plane, k], recv_sem=scale_recv.at[plane, k],
            device_id={"pw": d}, device_id_type=MESH,
        )

    def send(plane, k, _):
        d = (me + n // 2 + k) % n
        for c in range(per_dest):
            lane = pl.ds(c * LANES, LANES)
            both, tops = [], []
            for ref in (res, loc):
                first = plane * rows * chunks + d * per_dest + c
                x = ref[pl.ds(first, rows, stride=chunks), :]
                top = jnp.max(jnp.abs(x), axis=0, keepdims=True)
                inv = jnp.where(top > 1e-30, TOP / jnp.maximum(top, 1e-30), 0.0)
                both.append(jnp.floor(x * inv + 0.5).astype(jnp.int32))
                tops.append(top * (1.0 / TOP))
            q = jnp.concatenate(both, axis=0).astype(jnp.int16)

            @pl.when(k != n // 2)
            def _():
                out_codes[plane, d, :, lane] = q
                for a in range(2):
                    out_scales[plane, d, pl.ds(a, 1), lane] = tops[a]

            @pl.when(k == n // 2)
            def _():
                codes[plane, me, :, lane] = q
                for a in range(2):
                    scales[plane, me, pl.ds(a, 1), lane] = tops[a]

        @pl.when(k != n // 2)
        def _():
            scale_copy(plane, k, d).start()
            code_copy(plane, k, d).start()

        return 0

    group = max(1, 16 // rows)

    def rows_copy(i):
        at = pl.ds(pl.multiple_of(i * group * rows, group * rows), group * rows)
        return pltpu.make_async_copy(pieces1.at[at], pieces_out.at[at], pieces_sem.at[i])

    def receive(plane, pieces):
        kinetic = kinetic_of(lattice[...])

        def arrive(k, _):
            d = (me + n // 2 + k) % n

            @pl.when(k != n // 2)
            def _():
                scale_copy(plane, k, d).wait()
                code_copy(plane, k, d).wait()

            return 0

        def columns(s):
            q = codes[plane, s].astype(jnp.int32).astype(jnp.float32)
            scale = scales[plane, s]
            corr = q[:rows] * scale[0:1]
            other = q[rows:] * scale[1:2]
            return jnp.concatenate([corr, kinetic * corr + other], axis=1)

        def unpack(i):
            both = jnp.concatenate([columns(i * group + j) for j in range(group)], axis=0)
            top = both.astype(jnp.bfloat16)
            at = pl.ds(pl.multiple_of(i * group * rows, group * rows), group * rows)
            pieces[at, : 2 * cols] = top
            pieces[at, 2 * cols :] = (both - top.astype(jnp.float32)).astype(jnp.bfloat16)
            if plane == 1:
                rows_copy(i).start()

        def in_turn(k, _):
            arrive(k, 0)
            unpack((me + 2 * n - n // 2 - k) % n)
            return 0

        def in_order(i, _):
            unpack(i)
            return 0

        if group == 1:
            lax.fori_loop(0, n, in_turn, 0)
        else:
            lax.fori_loop(0, n, arrive, 0)
            lax.fori_loop(0, n // group, in_order, 0)

    def keep(panel):
        return (keepers[panel] == band).astype(jnp.float32).astype(jnp.bfloat16)

    loads[0].wait()
    loads[1].wait()
    pl.semaphore_wait(barrier, n + 1)
    for i in range(3):
        at = pl.ds(pl.multiple_of(other_start + fetched[i] * part, part), part)
        masked[at, :] = masked[at, :] * keep(1 - core)
        sib_copy(i, fetched[i]).start()
    loads[2].wait()
    loads[3].wait()
    lax.fori_loop(0, n // 2, functools.partial(send, 0), 0)
    loads[4].wait()
    for i in range(3):
        sib_copy(i, fetched[i]).wait_recv()
        at = pl.ds(pl.multiple_of(own_start + fetched[i] * part, part), part)
        near = pl.ds(pl.multiple_of(fetched[i] * part, part), part)
        masked[at, :] = masked[at, :] * keep(core) + chip_sum[near, :]
        far_copy(i, fetched[i]).start()
    lax.fori_loop(n // 2, n, functools.partial(send, 0), 0)
    loads[5].wait()
    loads[6].wait()
    lax.fori_loop(0, n, functools.partial(send, 1), 0)
    for load in loads[7:]:
        load.wait()

    for i in range(3):
        far_copy(i, fetched[i]).wait_recv()
        at = pl.ds(pl.multiple_of(own_start + fetched[i] * part, part), part)
        near = pl.ds(pl.multiple_of(fetched[i] * part, part), part)
        vmat_ref[at, :] = masked[at, :] + far_sum[near, :]
        if i == 0:
            side_copy(fetched[0]).start()
        back_copy(i, own_start, fetched[i]).start()
    side_copy(fetched[0]).wait_send()
    side_copy(fetched[3]).wait_recv()
    back_copy(3, own_start, fetched[3]).start()

    receive(0, pieces0)
    for i in range(PARTS):
        back_copy(i, other_start, fetched[i]).wait_recv()
    stores = [
        pltpu.make_async_copy(src, dst, store_sem.at[i])
        for i, (src, dst) in enumerate(
            ((vmat_ref, vmat_out), (psi_sum, psi0_out), (hpsi_sum, hpsi0_out))
        )
    ]
    stores[0].start()

    def tile(j, _):
        at = pl.ds(pl.multiple_of(j * TILE, TILE), TILE)
        total = rotated(vmat_ref[:, at], pieces0[...])
        psi_sum[at, :] = (psi_sum[at, :].astype(jnp.float32) + total[:, :cols]).astype(jnp.bfloat16)
        hpsi_sum[at, :] = (hpsi_sum[at, :].astype(jnp.float32) + total[:, cols:]).astype(jnp.bfloat16)
        return 0

    lax.fori_loop(0, vmat_ref.shape[1] // TILE, tile, 0)
    stores[1].start()
    stores[2].start()

    receive(1, pieces1)
    for i in range(3):
        sib_copy(i, fetched[i]).wait_send()
        far_copy(i, fetched[i]).wait_send()
    for i in range(PARTS):
        back_copy(i, own_start, fetched[i]).wait_send()
    for store in stores:
        store.wait()
    for i in range(n // group):
        rows_copy(i).wait()


def exchange(n, keepers, res, loc, store, lattice, psi, hpsi):
    planes, rows, _, width = res.shape
    chunks = width // LANES
    depth, span = store.shape[1:]
    cols = width // n
    flat = (planes * rows * chunks, LANES)
    dma = pltpu.SemaphoreType.DMA
    hbm = pl.BlockSpec(memory_space=pltpu.HBM)
    parts = jax.ShapeDtypeStruct((depth, 4 * cols), jnp.bfloat16)
    plane = jax.ShapeDtypeStruct((span, cols), jnp.bfloat16)
    return pl.pallas_call(
        functools.partial(exchange_kernel, n, rows, chunks),
        out_shape=(
            jax.ShapeDtypeStruct((depth, span), jnp.bfloat16), parts, plane, plane,
        ),
        in_specs=[hbm] * 7,
        out_specs=(hbm,) * 4,
        scratch_shapes=[
            pltpu.SMEM((2,), jnp.int32),
            pltpu.VMEM(flat, jnp.float32),
            pltpu.VMEM(flat, jnp.float32),
            pltpu.VMEM((depth, span), jnp.bfloat16),
            pltpu.VMEM(lattice.shape, jnp.int32),
            pltpu.VMEM((span, cols), jnp.bfloat16),
            pltpu.VMEM((span, cols), jnp.bfloat16),
            pltpu.VMEM((depth, span), jnp.bfloat16),
            pltpu.VMEM((planes, n, 2 * rows, cols), jnp.int16),
            pltpu.VMEM((planes, n, 8, cols), jnp.float32),
            pltpu.VMEM((planes, n, 2 * rows, cols), jnp.int16),
            pltpu.VMEM((planes, n, 8, cols), jnp.float32),
            pltpu.VMEM((depth // 2, span), jnp.bfloat16),
            pltpu.VMEM((depth // 2, span), jnp.bfloat16),
            pltpu.VMEM((depth, 4 * cols), jnp.bfloat16),
            pltpu.VMEM((depth, 4 * cols), jnp.bfloat16),
            dma((10,)), dma((3,)), dma((n,)), dma((planes, n)), dma((planes, n)), dma((planes, n)), dma((planes, n)),
            dma((3,)), dma((3,)), dma((3,)), dma((3,)), dma, dma,
            dma((PARTS,)), dma((PARTS,)),
        ],
        compiler_params=pltpu.CompilerParams(
            collective_id=0, has_side_effects=True, vmem_limit_bytes=GRANT
        ),
    )(
        keepers, res.reshape(flat), loc.reshape(flat), store.reshape(depth, span),
        lattice, psi, hpsi,
    )


def rotate_kernel(
    vmat_hbm, pieces_hbm, psi0_hbm, hpsi0_hbm, psi_hbm, hpsi_hbm,
    psi_out, hpsi_out,
    vmat, pieces, psi, hpsi, psi0, hpsi0,
    pieces_sem, vmat_sem, psi_sem, hpsi_sem, psi_out_sem, hpsi_out_sem, first_sem, first_out_sem,
):
    span, cols = psi.shape
    tiles = span // TILE

    def tile(j):
        return pl.ds(pl.multiple_of(j * TILE, TILE), TILE)

    def loads(j):
        at = tile(j)
        return (
            pltpu.make_async_copy(vmat_hbm.at[:, at], vmat.at[:, at], vmat_sem.at[j]),
            pltpu.make_async_copy(psi_hbm.at[1, at], psi.at[at], psi_sem.at[j]),
            pltpu.make_async_copy(hpsi_hbm.at[1, at], hpsi.at[at], hpsi_sem.at[j]),
        )

    def stores(j):
        at = tile(j)
        return (
            pltpu.make_async_copy(psi.at[at], psi_out.at[1, at], psi_out_sem.at[j]),
            pltpu.make_async_copy(hpsi.at[at], hpsi_out.at[1, at], hpsi_out_sem.at[j]),
        )

    load_pieces = pltpu.make_async_copy(pieces_hbm, pieces, pieces_sem)
    first_in = (
        pltpu.make_async_copy(psi0_hbm, psi0, first_sem.at[0]),
        pltpu.make_async_copy(hpsi0_hbm, hpsi0, first_sem.at[1]),
    )
    first_out = (
        pltpu.make_async_copy(psi0, psi_out.at[0], first_out_sem.at[0]),
        pltpu.make_async_copy(hpsi0, hpsi_out.at[0], first_out_sem.at[1]),
    )
    load_pieces.start()
    for load in loads(0) + loads(1):
        load.start()
    for load in first_in:
        load.start()
    for j in range(2, tiles):
        for load in loads(j):
            load.start()
    load_pieces.wait()

    for j in range(tiles):
        for load in loads(j):
            load.wait()
        at = tile(j)
        total = rotated(vmat[:, at], pieces[...])
        psi[at, :] = (psi[at, :].astype(jnp.float32) + total[:, :cols]).astype(jnp.bfloat16)
        hpsi[at, :] = (hpsi[at, :].astype(jnp.float32) + total[:, cols:]).astype(jnp.bfloat16)
        for store in stores(j):
            store.start()
        if j == 0:
            for i in range(2):
                first_in[i].wait()
                first_out[i].start()
    for j in range(tiles):
        for store in stores(j):
            store.wait()
    for store in first_out:
        store.wait()


def rotate(vmat, pieces, psi0, hpsi0, psi, hpsi):
    depth, span = vmat.shape
    cols = psi0.shape[1]
    tiles = span // TILE
    dma = pltpu.SemaphoreType.DMA
    hbm = pl.BlockSpec(memory_space=pltpu.HBM)
    out = jax.ShapeDtypeStruct((2, span, cols), jnp.bfloat16)
    plane = pltpu.VMEM((span, cols), jnp.bfloat16)
    return pl.pallas_call(
        rotate_kernel,
        out_shape=(out, out),
        in_specs=[hbm] * 6,
        out_specs=(hbm, hbm),
        scratch_shapes=[
            pltpu.VMEM((depth, span), jnp.bfloat16),
            pltpu.VMEM((depth, 4 * cols), jnp.bfloat16),
            plane, plane, plane, plane,
            dma, dma((tiles,)), dma((tiles,)), dma((tiles,)), dma((tiles,)), dma((tiles,)),
            dma((2,)), dma((2,)),
        ],
        compiler_params=pltpu.CompilerParams(vmem_limit_bytes=GRANT),
    )(vmat, pieces, psi0, hpsi0, psi, hpsi)


def per_device(n, res, loc, psi, hpsi, store, keepers, lattice):
    planes, span, _, cols = psi.shape
    psi_in, hpsi_in = (x.reshape(planes, span, cols) for x in (psi, hpsi))
    vmat, pieces, psi0, hpsi0 = exchange(
        n, keepers, res, loc, store, lattice, psi_in, hpsi_in
    )
    psi_new, hpsi_new = rotate(vmat, pieces, psi0, hpsi0, psi_in, hpsi_in)
    return psi_new.reshape(psi.shape), hpsi_new.reshape(hpsi.shape)


def solution(mesh):
    in_specs = (
        P(None, "pw", "band", None),
        P(None, "pw", "band", None),
        P(None, None, "band", "pw"),
        P(None, None, "band", "pw"),
        P("band", None, None),
        P(),
        P("band", "pw"),
    )
    out_specs = (P(None, None, "band", "pw"), P(None, None, "band", "pw"))
    return jax.shard_map(
        functools.partial(per_device, mesh.shape["pw"]),
        mesh=mesh, in_specs=in_specs, out_specs=out_specs, check_vma=False,
    )
```

```python
import functools

import jax
import jax.numpy as jnp
from jax import lax
from jax.experimental import pallas as pl
from jax.experimental.pallas import tpu as pltpu
from jax.sharding import PartitionSpec as P

GRID = 64
LANES = 128
PARTS = 4
TOP = 32766.0
TILE = 512
GRANT = 52 * 2**20
MESH = pl.DeviceIdType.MESH


def kinetic_of(lattice_position):
    first = lattice_position // (GRID * GRID)
    second = lattice_position // GRID % GRID
    third = lattice_position % GRID
    total = jnp.zeros(lattice_position.shape, jnp.int32)
    for index in (first, second, third):
        folded = jnp.where(index >= GRID // 2, index - GRID, index)
        total = total + folded * folded
    return total.astype(jnp.float32) / (GRID * GRID)


def rotated(v, pieces):
    dims = (((0,), (0,)), ((), ()))
    total = lax.dot_general(v, pieces, dims, preferred_element_type=jnp.float32)
    width = total.shape[1] // 2
    return total[:, :width] + total[:, width:]


def exchange_kernel(
    n, rows, chunks,
    keepers_hbm, res_hbm, loc_hbm, store_hbm, lattice_hbm, psi_hbm, hpsi_hbm,
    vmat_out, pieces1, psi_sum, hpsi_sum, psi1, hpsi1,
    keepers, res, loc, masked, lattice, vmat_ref,
    out_codes, out_scales, codes, scales, chip_sum, far_sum, pieces0,
    load_sem, store_sem, code_send, code_recv, scale_send, scale_recv,
    sib_send, sib_recv, far_send, far_recv, side_send, side_recv, back_send, back_recv,
):
    me = lax.axis_index("pw")
    band = lax.axis_index("band")
    core = band % 2
    side = band // 2
    sibling = side * 2 + (1 - core)
    across = (1 - side) * 2 + core
    parity = me % 2
    beside = me + 1 - 2 * parity
    per_dest = chunks // n
    cols = per_dest * LANES
    half = masked.shape[0] // 2
    part = half // PARTS
    own_start = pl.multiple_of(core * half, half)
    other_start = pl.multiple_of((1 - core) * half, half)

    plane_rows = rows * chunks
    first, second = pl.ds(0, plane_rows), pl.ds(plane_rows, plane_rows)
    other, mine = pl.ds(other_start, half), pl.ds(own_start, half)
    loads = [
        pltpu.make_async_copy(src, dst, load_sem.at[i])
        for i, (src, dst) in enumerate(
            (
                (keepers_hbm, keepers),
                (store_hbm.at[other], masked.at[other]),
                (res_hbm.at[first], res.at[first]),
                (loc_hbm.at[first], loc.at[first]),
                (store_hbm.at[mine], masked.at[mine]),
                (res_hbm.at[second], res.at[second]),
                (loc_hbm.at[second], loc.at[second]),
                (lattice_hbm, lattice),
                (psi_hbm.at[0], psi_sum),
                (hpsi_hbm.at[0], hpsi_sum),
                (psi_hbm.at[1], psi1),
                (hpsi_hbm.at[1], hpsi1),
            )
        )
    ]
    for load in loads:
        load.start()

    barrier = pltpu.get_barrier_semaphore()

    def greet(k, _):
        d = (me + 1 + k) % n
        pl.semaphore_signal(barrier, inc=1, device_id={"pw": d}, device_id_type=MESH)
        return 0

    lax.fori_loop(0, n - 1, greet, 0)
    for peer in (sibling, across):
        pl.semaphore_signal(barrier, inc=1, device_id={"band": peer}, device_id_type=MESH)
    out_scales[...] = jnp.zeros_like(out_scales)

    def sib_copy(i, q):
        return pltpu.make_async_remote_copy(
            src_ref=masked.at[pl.ds(other_start + q * part, part)],
            dst_ref=chip_sum.at[pl.ds(q * part, part)],
            send_sem=sib_send.at[i], recv_sem=sib_recv.at[i],
            device_id={"band": sibling}, device_id_type=MESH,
        )

    def far_copy(i, q):
        return pltpu.make_async_remote_copy(
            src_ref=masked.at[pl.ds(own_start + q * part, part)],
            dst_ref=far_sum.at[pl.ds(q * part, part)],
            send_sem=far_send.at[i], recv_sem=far_recv.at[i],
            device_id={"band": across}, device_id_type=MESH,
        )

    def side_copy(q):
        at = pl.ds(own_start + q * part, part)
        return pltpu.make_async_remote_copy(
            src_ref=vmat_ref.at[at], dst_ref=vmat_ref.at[at],
            send_sem=side_send, recv_sem=side_recv,
            device_id={"pw": beside}, device_id_type=MESH,
        )

    def back_copy(i, start, q):
        at = pl.ds(start + q * part, part)
        return pltpu.make_async_remote_copy(
            src_ref=vmat_ref.at[at], dst_ref=vmat_ref.at[at],
            send_sem=back_send.at[i], recv_sem=back_recv.at[i],
            device_id={"band": sibling}, device_id_type=MESH,
        )

    fetched = (2 + parity, 0, 1, 3 - parity)

    def code_copy(plane, k, d):
        return pltpu.make_async_remote_copy(
            src_ref=out_codes.at[plane, d], dst_ref=codes.at[plane, me],
            send_sem=code_send.at[plane, k], recv_sem=code_recv.at[plane, k],
            device_id={"pw": d}, device_id_type=MESH,
        )

    def scale_copy(plane, k, d):
        return pltpu.make_async_remote_copy(
            src_ref=out_scales.at[plane, d], dst_ref=scales.at[plane, me],
            send_sem=scale_send.at[plane, k], recv_sem=scale_recv.at[plane, k],
            device_id={"pw": d}, device_id_type=MESH,
        )

    def send(plane, k, _):
        d = (me + n // 2 + k) % n
        for c in range(per_dest):
            lane = pl.ds(c * LANES, LANES)
            both, tops = [], []
            for ref in (res, loc):
                first = plane * rows * chunks + d * per_dest + c
                x = ref[pl.ds(first, rows, stride=chunks), :]
                top = jnp.max(jnp.abs(x), axis=0, keepdims=True)
                inv = jnp.where(top > 1e-30, TOP / jnp.maximum(top, 1e-30), 0.0)
                both.append(jnp.floor(x * inv + 0.5).astype(jnp.int32))
                tops.append(top * (1.0 / TOP))
            q = jnp.concatenate(both, axis=0).astype(jnp.int16)

            @pl.when(k != n // 2)
            def _():
                out_codes[plane, d, :, lane] = q
                for a in range(2):
                    out_scales[plane, d, pl.ds(a, 1), lane] = tops[a]

            @pl.when(k == n // 2)
            def _():
                codes[plane, me, :, lane] = q
                for a in range(2):
                    scales[plane, me, pl.ds(a, 1), lane] = tops[a]

        @pl.when(k != n // 2)
        def _():
            if plane == 1:
                code_copy(0, k, d).wait_send()
            scale_copy(plane, k, d).start()
            code_copy(plane, k, d).start()

        return 0

    group = max(1, 16 // rows)

    def receive(plane, pieces):
        kinetic = kinetic_of(lattice[...])

        def arrive(k, _):
            d = (me + n // 2 + k) % n

            @pl.when(k != n // 2)
            def _():
                scale_copy(plane, k, d).wait()
                code_copy(plane, k, d).wait_recv()
                if plane == 1:
                    code_copy(plane, k, d).wait_send()

            return 0

        def columns(s):
            q = codes[plane, s].astype(jnp.int32).astype(jnp.float32)
            scale = scales[plane, s]
            corr = q[:rows] * scale[0:1]
            other = q[rows:] * scale[1:2]
            return jnp.concatenate([corr, kinetic * corr + other], axis=1)

        def unpack(i):
            both = jnp.concatenate([columns(i * group + j) for j in range(group)], axis=0)
            top = both.astype(jnp.bfloat16)
            at = pl.ds(pl.multiple_of(i * group * rows, group * rows), group * rows)
            pieces[at, : 2 * cols] = top
            pieces[at, 2 * cols :] = (both - top.astype(jnp.float32)).astype(jnp.bfloat16)

        def in_turn(k, _):
            arrive(k, 0)
            unpack((me + 2 * n - n // 2 - k) % n)
            return 0

        def in_order(i, _):
            unpack(i)
            return 0

        if group == 1:
            lax.fori_loop(0, n, in_turn, 0)
        else:
            lax.fori_loop(0, n, arrive, 0)
            lax.fori_loop(0, n // group, in_order, 0)

    def keep(panel):
        return (keepers[panel] == band).astype(jnp.float32).astype(jnp.bfloat16)

    loads[0].wait()
    loads[1].wait()
    pl.semaphore_wait(barrier, n + 1)
    for i in range(3):
        at = pl.ds(pl.multiple_of(other_start + fetched[i] * part, part), part)
        masked[at, :] = masked[at, :] * keep(1 - core)
        sib_copy(i, fetched[i]).start()
    loads[2].wait()
    loads[3].wait()
    lax.fori_loop(0, n // 2, functools.partial(send, 0), 0)
    loads[4].wait()
    for i in range(3):
        sib_copy(i, fetched[i]).wait_recv()
        at = pl.ds(pl.multiple_of(own_start + fetched[i] * part, part), part)
        near = pl.ds(pl.multiple_of(fetched[i] * part, part), part)
        masked[at, :] = masked[at, :] * keep(core) + chip_sum[near, :]
        far_copy(i, fetched[i]).start()
    lax.fori_loop(n // 2, n, functools.partial(send, 0), 0)
    loads[5].wait()
    loads[6].wait()
    for load in loads[7:]:
        load.wait()

    lax.fori_loop(0, n // 2, functools.partial(send, 1), 0)
    for i in range(3):
        if i == 1:
            lax.fori_loop(n // 2, n, functools.partial(send, 1), 0)
        far_copy(i, fetched[i]).wait_recv()
        at = pl.ds(pl.multiple_of(own_start + fetched[i] * part, part), part)
        near = pl.ds(pl.multiple_of(fetched[i] * part, part), part)
        vmat_ref[at, :] = masked[at, :] + far_sum[near, :]
        if i == 0:
            side_copy(fetched[0]).start()
        back_copy(i, own_start, fetched[i]).start()
    side_copy(fetched[0]).wait_send()
    side_copy(fetched[3]).wait_recv()
    back_copy(3, own_start, fetched[3]).start()

    receive(0, pieces0)
    for i in range(PARTS):
        back_copy(i, other_start, fetched[i]).wait_recv()
    store = pltpu.make_async_copy(vmat_ref, vmat_out, store_sem)
    store.start()
    def tile(j, _):
        at = pl.ds(pl.multiple_of(j * TILE, TILE), TILE)
        total = rotated(vmat_ref[:, at], pieces0[...])
        psi_sum[at, :] = (psi_sum[at, :].astype(jnp.float32) + total[:, :cols]).astype(jnp.bfloat16)
        hpsi_sum[at, :] = (hpsi_sum[at, :].astype(jnp.float32) + total[:, cols:]).astype(jnp.bfloat16)
        return 0

    lax.fori_loop(0, vmat_ref.shape[1] // TILE, tile, 0)

    receive(1, pieces1)
    for i in range(3):
        sib_copy(i, fetched[i]).wait_send()
        far_copy(i, fetched[i]).wait_send()
    for i in range(PARTS):
        back_copy(i, own_start, fetched[i]).wait_send()
    store.wait()


def exchange(n, keepers, res, loc, store, lattice, psi, hpsi):
    planes, rows, _, width = res.shape
    chunks = width // LANES
    depth, span = store.shape[1:]
    cols = width // n
    flat = (planes * rows * chunks, LANES)
    dma = pltpu.SemaphoreType.DMA
    hbm = pl.BlockSpec(memory_space=pltpu.HBM)
    parts = jax.ShapeDtypeStruct((depth, 4 * cols), jnp.bfloat16)
    plane = jax.ShapeDtypeStruct((span, cols), jnp.bfloat16)
    return pl.pallas_call(
        functools.partial(exchange_kernel, n, rows, chunks),
        out_shape=(
            jax.ShapeDtypeStruct((depth, span), jnp.bfloat16), parts, plane, plane, plane, plane,
        ),
        in_specs=[hbm] * 7,
        out_specs=(hbm,) + (pl.BlockSpec(memory_space=pltpu.VMEM),) * 5,
        scratch_shapes=[
            pltpu.SMEM((2,), jnp.int32),
            pltpu.VMEM(flat, jnp.float32),
            pltpu.VMEM(flat, jnp.float32),
            pltpu.VMEM((depth, span), jnp.bfloat16),
            pltpu.VMEM(lattice.shape, jnp.int32),
            pltpu.VMEM((depth, span), jnp.bfloat16),
            pltpu.VMEM((planes, n, 2 * rows, cols), jnp.int16),
            pltpu.VMEM((planes, n, 8, cols), jnp.float32),
            pltpu.VMEM((planes, n, 2 * rows, cols), jnp.int16),
            pltpu.VMEM((planes, n, 8, cols), jnp.float32),
            pltpu.VMEM((depth // 2, span), jnp.bfloat16),
            pltpu.VMEM((depth // 2, span), jnp.bfloat16),
            pltpu.VMEM((depth, 4 * cols), jnp.bfloat16),
            dma((12,)), dma, dma((planes, n)), dma((planes, n)), dma((planes, n)), dma((planes, n)),
            dma((3,)), dma((3,)), dma((3,)), dma((3,)), dma, dma,
            dma((PARTS,)), dma((PARTS,)),
        ],
        compiler_params=pltpu.CompilerParams(
            collective_id=0, has_side_effects=True, vmem_limit_bytes=GRANT
        ),
    )(
        keepers, res.reshape(flat), loc.reshape(flat), store.reshape(depth, span),
        lattice, psi, hpsi,
    )


def rotate_kernel(
    vmat_hbm, pieces, psi0, hpsi0, psi1, hpsi1, psi_out, hpsi_out,
    vmat, psi, hpsi, vmat_sem, psi_sem, hpsi_sem, first_sem,
):
    span, cols = psi.shape
    tiles = span // TILE
    first = (
        pltpu.make_async_copy(psi0, psi_out.at[0], first_sem.at[0]),
        pltpu.make_async_copy(hpsi0, hpsi_out.at[0], first_sem.at[1]),
    )
    loads = []
    for j in range(tiles):
        at = pl.ds(j * TILE, TILE)
        loads.append(pltpu.make_async_copy(vmat_hbm.at[:, at], vmat.at[:, at], vmat_sem.at[j]))
        loads[-1].start()
    for store in first:
        store.start()
    stores = []
    for j in range(tiles):
        at = pl.ds(j * TILE, TILE)
        loads[j].wait()
        total = rotated(vmat[:, at], pieces[...])
        psi[at, :] = (psi1[at, :].astype(jnp.float32) + total[:, :cols]).astype(jnp.bfloat16)
        hpsi[at, :] = (hpsi1[at, :].astype(jnp.float32) + total[:, cols:]).astype(jnp.bfloat16)
        stores += [
            pltpu.make_async_copy(psi.at[at], psi_out.at[1, at], psi_sem.at[j]),
            pltpu.make_async_copy(hpsi.at[at], hpsi_out.at[1, at], hpsi_sem.at[j]),
        ]
        for store in stores[-2:]:
            store.start()
    for store in stores:
        store.wait()
    for store in first:
        store.wait()


def rotate(vmat, pieces, psi0, hpsi0, psi1, hpsi1):
    span, cols = psi0.shape
    tiles = span // TILE
    dma = pltpu.SemaphoreType.DMA
    hbm = pl.BlockSpec(memory_space=pltpu.HBM)
    out = jax.ShapeDtypeStruct((2, span, cols), jnp.bfloat16)
    plane = pltpu.VMEM((span, cols), jnp.bfloat16)
    return pl.pallas_call(
        rotate_kernel,
        out_shape=(out, out),
        in_specs=[hbm] + [pl.BlockSpec(memory_space=pltpu.VMEM)] * 5,
        out_specs=(hbm, hbm),
        scratch_shapes=[
            pltpu.VMEM(vmat.shape, vmat.dtype), plane, plane,
            dma((tiles,)), dma((tiles,)), dma((tiles,)), dma((2,)),
        ],
        compiler_params=pltpu.CompilerParams(vmem_limit_bytes=GRANT),
    )(vmat, pieces, psi0, hpsi0, psi1, hpsi1)


def per_device(n, res, loc, psi, hpsi, store, keepers, lattice):
    planes, span, _, cols = psi.shape
    psi_in, hpsi_in = (x.reshape(planes, span, cols) for x in (psi, hpsi))
    handed = exchange(n, keepers, res, loc, store, lattice, psi_in, hpsi_in)
    psi_new, hpsi_new = rotate(*handed)
    return psi_new.reshape(psi.shape), hpsi_new.reshape(hpsi.shape)


def solution(mesh):
    in_specs = (
        P(None, "pw", "band", None),
        P(None, "pw", "band", None),
        P(None, None, "band", "pw"),
        P(None, None, "band", "pw"),
        P("band", None, None),
        P(),
        P("band", "pw"),
    )
    out_specs = (P(None, None, "band", "pw"), P(None, None, "band", "pw"))
    return jax.shard_map(
        functools.partial(per_device, mesh.shape["pw"]),
        mesh=mesh, in_specs=in_specs, out_specs=out_specs, check_vma=False,
    )
```

```python
import functools

import jax
import jax.numpy as jnp
from jax import lax
from jax.experimental import pallas as pl
from jax.experimental.pallas import tpu as pltpu
from jax.sharding import PartitionSpec as P

GRID = 64
LANES = 128
PARTS = 4
TOP = 32766.0
TILE = 512
GRANT = 48 * 2**20
MESH = pl.DeviceIdType.MESH


def kinetic_of(lattice_position):
    first = lattice_position // (GRID * GRID)
    second = lattice_position // GRID % GRID
    third = lattice_position % GRID
    total = jnp.zeros(lattice_position.shape, jnp.int32)
    for index in (first, second, third):
        folded = jnp.where(index >= GRID // 2, index - GRID, index)
        total = total + folded * folded
    return total.astype(jnp.float32) / (GRID * GRID)


def rotated(v, pieces):
    dims = (((0,), (0,)), ((), ()))
    total = lax.dot_general(v, pieces, dims, preferred_element_type=jnp.float32)
    width = total.shape[1] // 2
    return total[:, :width] + total[:, width:]


def exchange_kernel(
    n, rows, chunks,
    keepers_hbm, res_hbm, loc_hbm, store_hbm, lattice_hbm, psi_hbm, hpsi_hbm,
    vmat_out, pieces1, psi_sum, hpsi_sum, psi1, hpsi1,
    keepers, res, loc, masked, lattice, vmat_ref,
    out_codes, out_scales, codes, scales, chip_sum, far_sum, pieces0,
    load_sem, store_sem, code_send, code_recv, scale_send, scale_recv,
    sib_send, sib_recv, far_send, far_recv, side_send, side_recv, back_send, back_recv,
):
    me = lax.axis_index("pw")
    band = lax.axis_index("band")
    core = band % 2
    side = band // 2
    sibling = side * 2 + (1 - core)
    across = (1 - side) * 2 + core
    parity = me % 2
    beside = me + 1 - 2 * parity
    per_dest = chunks // n
    cols = per_dest * LANES
    half = masked.shape[0] // 2
    part = half // PARTS
    own_start = pl.multiple_of(core * half, half)
    other_start = pl.multiple_of((1 - core) * half, half)

    plane_rows = rows * chunks
    first, second = pl.ds(0, plane_rows), pl.ds(plane_rows, plane_rows)
    other, mine = pl.ds(other_start, half), pl.ds(own_start, half)
    loads = [
        pltpu.make_async_copy(src, dst, load_sem.at[i])
        for i, (src, dst) in enumerate(
            (
                (keepers_hbm, keepers),
                (store_hbm.at[other], masked.at[other]),
                (res_hbm.at[first], res.at[first]),
                (loc_hbm.at[first], loc.at[first]),
                (store_hbm.at[mine], masked.at[mine]),
                (res_hbm.at[second], res.at[second]),
                (loc_hbm.at[second], loc.at[second]),
                (lattice_hbm, lattice),
                (psi_hbm.at[0], psi_sum),
                (hpsi_hbm.at[0], hpsi_sum),
                (psi_hbm.at[1], psi1),
                (hpsi_hbm.at[1], hpsi1),
            )
        )
    ]
    for load in loads:
        load.start()

    barrier = pltpu.get_barrier_semaphore()

    def greet(k, _):
        d = (me + 1 + k) % n
        pl.semaphore_signal(barrier, inc=1, device_id={"pw": d}, device_id_type=MESH)
        return 0

    lax.fori_loop(0, n - 1, greet, 0)
    for peer in (sibling, across):
        pl.semaphore_signal(barrier, inc=1, device_id={"band": peer}, device_id_type=MESH)
    out_scales[...] = jnp.zeros_like(out_scales)

    def sib_copy(i, q):
        return pltpu.make_async_remote_copy(
            src_ref=masked.at[pl.ds(other_start + q * part, part)],
            dst_ref=chip_sum.at[pl.ds(q * part, part)],
            send_sem=sib_send.at[i], recv_sem=sib_recv.at[i],
            device_id={"band": sibling}, device_id_type=MESH,
        )

    def far_copy(i, q):
        return pltpu.make_async_remote_copy(
            src_ref=masked.at[pl.ds(own_start + q * part, part)],
            dst_ref=far_sum.at[pl.ds(q * part, part)],
            send_sem=far_send.at[i], recv_sem=far_recv.at[i],
            device_id={"band": across}, device_id_type=MESH,
        )

    def side_copy(q):
        at = pl.ds(own_start + q * part, part)
        return pltpu.make_async_remote_copy(
            src_ref=vmat_ref.at[at], dst_ref=vmat_ref.at[at],
            send_sem=side_send, recv_sem=side_recv,
            device_id={"pw": beside}, device_id_type=MESH,
        )

    def back_copy(i, start, q):
        at = pl.ds(start + q * part, part)
        return pltpu.make_async_remote_copy(
            src_ref=vmat_ref.at[at], dst_ref=vmat_ref.at[at],
            send_sem=back_send.at[i], recv_sem=back_recv.at[i],
            device_id={"band": sibling}, device_id_type=MESH,
        )

    fetched = (2 + parity, 0, 1, 3 - parity)

    def code_copy(plane, k, d):
        return pltpu.make_async_remote_copy(
            src_ref=out_codes.at[plane, d], dst_ref=codes.at[plane, me],
            send_sem=code_send.at[plane, k], recv_sem=code_recv.at[plane, k],
            device_id={"pw": d}, device_id_type=MESH,
        )

    def scale_copy(plane, k, d):
        return pltpu.make_async_remote_copy(
            src_ref=out_scales.at[plane, d], dst_ref=scales.at[plane, me],
            send_sem=scale_send.at[plane, k], recv_sem=scale_recv.at[plane, k],
            device_id={"pw": d}, device_id_type=MESH,
        )

    def send(plane, k, _):
        d = (me + n // 2 + k) % n
        for c in range(per_dest):
            lane = pl.ds(c * LANES, LANES)
            both, tops = [], []
            for ref in (res, loc):
                first = plane * rows * chunks + d * per_dest + c
                x = ref[pl.ds(first, rows, stride=chunks), :]
                top = jnp.max(jnp.abs(x), axis=0, keepdims=True)
                inv = jnp.where(top > 1e-30, TOP / jnp.maximum(top, 1e-30), 0.0)
                both.append(jnp.floor(x * inv + 0.5).astype(jnp.int32))
                tops.append(top * (1.0 / TOP))
            q = jnp.concatenate(both, axis=0).astype(jnp.int16)

            @pl.when(k != n // 2)
            def _():
                out_codes[plane, d, :, lane] = q
                for a in range(2):
                    out_scales[plane, d, pl.ds(a, 1), lane] = tops[a]

            @pl.when(k == n // 2)
            def _():
                codes[plane, me, :, lane] = q
                for a in range(2):
                    scales[plane, me, pl.ds(a, 1), lane] = tops[a]

        @pl.when(k != n // 2)
        def _():
            scale_copy(plane, k, d).start()
            code_copy(plane, k, d).start()

        return 0

    group = max(1, 16 // rows)

    def receive(plane, pieces):
        kinetic = kinetic_of(lattice[...])

        def arrive(k, _):
            d = (me + n // 2 + k) % n

            @pl.when(k != n // 2)
            def _():
                scale_copy(plane, k, d).wait()
                code_copy(plane, k, d).wait()

            return 0

        def columns(s):
            q = codes[plane, s].astype(jnp.int32).astype(jnp.float32)
            scale = scales[plane, s]
            corr = q[:rows] * scale[0:1]
            other = q[rows:] * scale[1:2]
            return jnp.concatenate([corr, kinetic * corr + other], axis=1)

        def unpack(i):
            both = jnp.concatenate([columns(i * group + j) for j in range(group)], axis=0)
            top = both.astype(jnp.bfloat16)
            at = pl.ds(pl.multiple_of(i * group * rows, group * rows), group * rows)
            pieces[at, : 2 * cols] = top
            pieces[at, 2 * cols :] = (both - top.astype(jnp.float32)).astype(jnp.bfloat16)

        def in_turn(k, _):
            arrive(k, 0)
            unpack((me + 2 * n - n // 2 - k) % n)
            return 0

        def in_order(i, _):
            unpack(i)
            return 0

        if group == 1:
            lax.fori_loop(0, n, in_turn, 0)
        else:
            lax.fori_loop(0, n, arrive, 0)
            lax.fori_loop(0, n // group, in_order, 0)

    def keep(panel):
        return (keepers[panel] == band).astype(jnp.float32).astype(jnp.bfloat16)

    loads[0].wait()
    loads[1].wait()
    pl.semaphore_wait(barrier, n + 1)
    for i in range(3):
        at = pl.ds(pl.multiple_of(other_start + fetched[i] * part, part), part)
        masked[at, :] = masked[at, :] * keep(1 - core)
        sib_copy(i, fetched[i]).start()
    loads[2].wait()
    loads[3].wait()
    lax.fori_loop(0, n // 2, functools.partial(send, 0), 0)
    loads[4].wait()
    for i in range(3):
        sib_copy(i, fetched[i]).wait_recv()
        at = pl.ds(pl.multiple_of(own_start + fetched[i] * part, part), part)
        near = pl.ds(pl.multiple_of(fetched[i] * part, part), part)
        masked[at, :] = masked[at, :] * keep(core) + chip_sum[near, :]
        far_copy(i, fetched[i]).start()
    lax.fori_loop(n // 2, n, functools.partial(send, 0), 0)
    loads[5].wait()
    loads[6].wait()
    lax.fori_loop(0, n, functools.partial(send, 1), 0)
    for load in loads[7:]:
        load.wait()

    for i in range(3):
        far_copy(i, fetched[i]).wait_recv()
        at = pl.ds(pl.multiple_of(own_start + fetched[i] * part, part), part)
        near = pl.ds(pl.multiple_of(fetched[i] * part, part), part)
        vmat_ref[at, :] = masked[at, :] + far_sum[near, :]
        if i == 0:
            side_copy(fetched[0]).start()
        back_copy(i, own_start, fetched[i]).start()
    side_copy(fetched[0]).wait_send()
    side_copy(fetched[3]).wait_recv()
    back_copy(3, own_start, fetched[3]).start()

    receive(0, pieces0)
    for i in range(PARTS):
        back_copy(i, other_start, fetched[i]).wait_recv()
    store = pltpu.make_async_copy(vmat_ref, vmat_out, store_sem)
    store.start()
    def tile(j, _):
        at = pl.ds(pl.multiple_of(j * TILE, TILE), TILE)
        total = rotated(vmat_ref[:, at], pieces0[...])
        psi_sum[at, :] = (psi_sum[at, :].astype(jnp.float32) + total[:, :cols]).astype(jnp.bfloat16)
        hpsi_sum[at, :] = (hpsi_sum[at, :].astype(jnp.float32) + total[:, cols:]).astype(jnp.bfloat16)
        return 0

    lax.fori_loop(0, vmat_ref.shape[1] // TILE, tile, 0)

    receive(1, pieces1)
    for i in range(3):
        sib_copy(i, fetched[i]).wait_send()
        far_copy(i, fetched[i]).wait_send()
    for i in range(PARTS):
        back_copy(i, own_start, fetched[i]).wait_send()
    store.wait()


def exchange(n, keepers, res, loc, store, lattice, psi, hpsi):
    planes, rows, _, width = res.shape
    chunks = width // LANES
    depth, span = store.shape[1:]
    cols = width // n
    flat = (planes * rows * chunks, LANES)
    dma = pltpu.SemaphoreType.DMA
    hbm = pl.BlockSpec(memory_space=pltpu.HBM)
    parts = jax.ShapeDtypeStruct((depth, 4 * cols), jnp.bfloat16)
    plane = jax.ShapeDtypeStruct((span, cols), jnp.bfloat16)
    return pl.pallas_call(
        functools.partial(exchange_kernel, n, rows, chunks),
        out_shape=(
            jax.ShapeDtypeStruct((depth, span), jnp.bfloat16), parts, plane, plane, plane, plane,
        ),
        in_specs=[hbm] * 7,
        out_specs=(hbm,) + (pl.BlockSpec(memory_space=pltpu.VMEM),) * 5,
        scratch_shapes=[
            pltpu.SMEM((2,), jnp.int32),
            pltpu.VMEM(flat, jnp.float32),
            pltpu.VMEM(flat, jnp.float32),
            pltpu.VMEM((depth, span), jnp.bfloat16),
            pltpu.VMEM(lattice.shape, jnp.int32),
            pltpu.VMEM((depth, span), jnp.bfloat16),
            pltpu.VMEM((planes, n, 2 * rows, cols), jnp.int16),
            pltpu.VMEM((planes, n, 8, cols), jnp.float32),
            pltpu.VMEM((planes, n, 2 * rows, cols), jnp.int16),
            pltpu.VMEM((planes, n, 8, cols), jnp.float32),
            pltpu.VMEM((depth // 2, span), jnp.bfloat16),
            pltpu.VMEM((depth // 2, span), jnp.bfloat16),
            pltpu.VMEM((depth, 4 * cols), jnp.bfloat16),
            dma((12,)), dma, dma((planes, n)), dma((planes, n)), dma((planes, n)), dma((planes, n)),
            dma((3,)), dma((3,)), dma((3,)), dma((3,)), dma, dma,
            dma((PARTS,)), dma((PARTS,)),
        ],
        compiler_params=pltpu.CompilerParams(
            collective_id=0, has_side_effects=True, vmem_limit_bytes=GRANT
        ),
    )(
        keepers, res.reshape(flat), loc.reshape(flat), store.reshape(depth, span),
        lattice, psi, hpsi,
    )


def rotate_kernel(
    vmat_hbm, pieces, psi0, hpsi0, psi1, hpsi1, psi_out, hpsi_out,
    vmat, psi, hpsi, vmat_sem, psi_sem, hpsi_sem, first_sem,
):
    span, cols = psi.shape
    tiles = span // TILE
    first = (
        pltpu.make_async_copy(psi0, psi_out.at[0], first_sem.at[0]),
        pltpu.make_async_copy(hpsi0, hpsi_out.at[0], first_sem.at[1]),
    )
    loads = []
    for j in range(tiles):
        at = pl.ds(j * TILE, TILE)
        loads.append(pltpu.make_async_copy(vmat_hbm.at[:, at], vmat.at[:, at], vmat_sem.at[j]))
        loads[-1].start()
    for store in first:
        store.start()
    stores = []
    for j in range(tiles):
        at = pl.ds(j * TILE, TILE)
        loads[j].wait()
        total = rotated(vmat[:, at], pieces[...])
        psi[at, :] = (psi1[at, :].astype(jnp.float32) + total[:, :cols]).astype(jnp.bfloat16)
        hpsi[at, :] = (hpsi1[at, :].astype(jnp.float32) + total[:, cols:]).astype(jnp.bfloat16)
        stores += [
            pltpu.make_async_copy(psi.at[at], psi_out.at[1, at], psi_sem.at[j]),
            pltpu.make_async_copy(hpsi.at[at], hpsi_out.at[1, at], hpsi_sem.at[j]),
        ]
        for store in stores[-2:]:
            store.start()
    for store in stores:
        store.wait()
    for store in first:
        store.wait()


def rotate(vmat, pieces, psi0, hpsi0, psi1, hpsi1):
    span, cols = psi0.shape
    tiles = span // TILE
    dma = pltpu.SemaphoreType.DMA
    hbm = pl.BlockSpec(memory_space=pltpu.HBM)
    out = jax.ShapeDtypeStruct((2, span, cols), jnp.bfloat16)
    plane = pltpu.VMEM((span, cols), jnp.bfloat16)
    return pl.pallas_call(
        rotate_kernel,
        out_shape=(out, out),
        in_specs=[hbm] + [pl.BlockSpec(memory_space=pltpu.VMEM)] * 5,
        out_specs=(hbm, hbm),
        scratch_shapes=[
            pltpu.VMEM(vmat.shape, vmat.dtype), plane, plane,
            dma((tiles,)), dma((tiles,)), dma((tiles,)), dma((2,)),
        ],
        compiler_params=pltpu.CompilerParams(vmem_limit_bytes=GRANT),
    )(vmat, pieces, psi0, hpsi0, psi1, hpsi1)


def per_device(n, res, loc, psi, hpsi, store, keepers, lattice):
    planes, span, _, cols = psi.shape
    psi_in, hpsi_in = (x.reshape(planes, span, cols) for x in (psi, hpsi))
    handed = exchange(n, keepers, res, loc, store, lattice, psi_in, hpsi_in)
    psi_new, hpsi_new = rotate(*handed)
    return psi_new.reshape(psi.shape), hpsi_new.reshape(hpsi.shape)


def solution(mesh):
    in_specs = (
        P(None, "pw", "band", None),
        P(None, "pw", "band", None),
        P(None, None, "band", "pw"),
        P(None, None, "band", "pw"),
        P("band", None, None),
        P(),
        P("band", "pw"),
    )
    out_specs = (P(None, None, "band", "pw"), P(None, None, "band", "pw"))
    return jax.shard_map(
        functools.partial(per_device, mesh.shape["pw"]),
        mesh=mesh, in_specs=in_specs, out_specs=out_specs, check_vma=False,
    )
```

```python
import functools

import jax
import jax.numpy as jnp
from jax import lax
from jax.experimental import pallas as pl
from jax.experimental.pallas import tpu as pltpu
from jax.sharding import PartitionSpec as P

GRID = 64
LANES = 128
PARTS = 4
TOP = 32766.0
TILE = 512
GRANT = 48 * 2**20
MESH = pl.DeviceIdType.MESH


def kinetic_of(lattice_position):
    first = lattice_position // (GRID * GRID)
    second = lattice_position // GRID % GRID
    third = lattice_position % GRID
    total = jnp.zeros(lattice_position.shape, jnp.int32)
    for index in (first, second, third):
        folded = jnp.where(index >= GRID // 2, index - GRID, index)
        total = total + folded * folded
    return total.astype(jnp.float32) / (GRID * GRID)


def rotated(v, pieces):
    dims = (((0,), (0,)), ((), ()))
    total = lax.dot_general(v, pieces, dims, preferred_element_type=jnp.float32)
    width = total.shape[1] // 2
    return total[:, :width] + total[:, width:]


def exchange_kernel(
    n, rows, chunks,
    lattice_hbm, res_hbm, loc_hbm, store_hbm, psi_hbm, hpsi_hbm,
    vmat_out, pieces1, psi_sum, hpsi_sum, psi1, hpsi1,
    lattice, res, loc, masked, vmat_ref,
    out_codes, out_scales, codes, scales, chip_sum, far_sum, pieces0,
    load_sem, store_sem, code_send, code_recv, scale_send, scale_recv,
    sib_send, sib_recv, far_send, far_recv, side_send, side_recv, back_send, back_recv,
):
    me = lax.axis_index("pw")
    band = lax.axis_index("band")
    core = band % 2
    side = band // 2
    sibling = side * 2 + (1 - core)
    across = (1 - side) * 2 + core
    parity = me % 2
    beside = me + 1 - 2 * parity
    per_dest = chunks // n
    cols = per_dest * LANES
    half = masked.shape[0] // 2
    part = half // PARTS
    own_start = pl.multiple_of(core * half, half)
    other_start = pl.multiple_of((1 - core) * half, half)

    plane_rows = rows * chunks
    first, second = pl.ds(0, plane_rows), pl.ds(plane_rows, plane_rows)
    other, mine = pl.ds(other_start, half), pl.ds(own_start, half)
    loads = [
        pltpu.make_async_copy(src, dst, load_sem.at[i])
        for i, (src, dst) in enumerate(
            (
                (lattice_hbm, lattice),
                (store_hbm.at[other], masked.at[other]),
                (res_hbm.at[first], res.at[first]),
                (loc_hbm.at[first], loc.at[first]),
                (store_hbm.at[mine], masked.at[mine]),
                (res_hbm.at[second], res.at[second]),
                (loc_hbm.at[second], loc.at[second]),
                (psi_hbm.at[0], psi_sum),
                (hpsi_hbm.at[0], hpsi_sum),
                (psi_hbm.at[1], psi1),
                (hpsi_hbm.at[1], hpsi1),
            )
        )
    ]
    for load in loads:
        load.start()

    barrier = pltpu.get_barrier_semaphore()

    def greet(k, _):
        d = (me + 1 + k) % n
        pl.semaphore_signal(barrier, inc=1, device_id={"pw": d}, device_id_type=MESH)
        return 0

    lax.fori_loop(0, n - 1, greet, 0)
    for peer in (sibling, across):
        pl.semaphore_signal(barrier, inc=1, device_id={"band": peer}, device_id_type=MESH)
    out_scales[...] = jnp.zeros_like(out_scales)

    def sib_copy(i, q):
        return pltpu.make_async_remote_copy(
            src_ref=masked.at[pl.ds(other_start + q * part, part)],
            dst_ref=chip_sum.at[pl.ds(q * part, part)],
            send_sem=sib_send.at[i], recv_sem=sib_recv.at[i],
            device_id={"band": sibling}, device_id_type=MESH,
        )

    def far_copy(i, q):
        return pltpu.make_async_remote_copy(
            src_ref=masked.at[pl.ds(own_start + q * part, part)],
            dst_ref=far_sum.at[pl.ds(q * part, part)],
            send_sem=far_send.at[i], recv_sem=far_recv.at[i],
            device_id={"band": across}, device_id_type=MESH,
        )

    def side_copy(q):
        at = pl.ds(own_start + q * part, part)
        return pltpu.make_async_remote_copy(
            src_ref=vmat_ref.at[at], dst_ref=vmat_ref.at[at],
            send_sem=side_send, recv_sem=side_recv,
            device_id={"pw": beside}, device_id_type=MESH,
        )

    def back_copy(i, start, q):
        at = pl.ds(start + q * part, part)
        return pltpu.make_async_remote_copy(
            src_ref=vmat_ref.at[at], dst_ref=vmat_ref.at[at],
            send_sem=back_send.at[i], recv_sem=back_recv.at[i],
            device_id={"band": sibling}, device_id_type=MESH,
        )

    fetched = (2 + parity, 0, 1, 3 - parity)

    def code_copy(plane, k, d):
        return pltpu.make_async_remote_copy(
            src_ref=out_codes.at[plane, d], dst_ref=codes.at[plane, me],
            send_sem=code_send.at[plane, k], recv_sem=code_recv.at[plane, k],
            device_id={"pw": d}, device_id_type=MESH,
        )

    def scale_copy(plane, k, d):
        return pltpu.make_async_remote_copy(
            src_ref=out_scales.at[plane, d], dst_ref=scales.at[plane, me],
            send_sem=scale_send.at[plane, k], recv_sem=scale_recv.at[plane, k],
            device_id={"pw": d}, device_id_type=MESH,
        )

    def send(plane, k, _):
        d = (me + n // 2 + k) % n
        for c in range(per_dest):
            lane = pl.ds(c * LANES, LANES)
            both, tops = [], []
            for ref in (res, loc):
                first = plane * rows * chunks + d * per_dest + c
                x = ref[pl.ds(first, rows, stride=chunks), :]
                top = jnp.max(jnp.abs(x), axis=0, keepdims=True)
                inv = jnp.where(top > 1e-30, TOP / jnp.maximum(top, 1e-30), 0.0)
                both.append(jnp.floor(x * inv + 0.5).astype(jnp.int32))
                tops.append(top * (1.0 / TOP))
            q = jnp.concatenate(both, axis=0).astype(jnp.int16)

            @pl.when(k != n // 2)
            def _():
                out_codes[plane, d, :, lane] = q
                for a in range(2):
                    out_scales[plane, d, pl.ds(a, 1), lane] = tops[a]

            @pl.when(k == n // 2)
            def _():
                codes[plane, me, :, lane] = q
                for a in range(2):
                    scales[plane, me, pl.ds(a, 1), lane] = tops[a]

        @pl.when(k != n // 2)
        def _():
            scale_copy(plane, k, d).start()
            code_copy(plane, k, d).start()

        return 0

    group = max(1, 16 // rows)

    def receive(plane, pieces):
        kinetic = kinetic_of(lattice[0:1, :])

        def arrive(k, _):
            d = (me + n // 2 + k) % n

            @pl.when(k != n // 2)
            def _():
                scale_copy(plane, k, d).wait()
                code_copy(plane, k, d).wait()

            return 0

        def columns(s):
            q = codes[plane, s].astype(jnp.int32).astype(jnp.float32)
            scale = scales[plane, s]
            corr = q[:rows] * scale[0:1]
            other = q[rows:] * scale[1:2]
            return jnp.concatenate([corr, kinetic * corr + other], axis=1)

        def unpack(i):
            both = jnp.concatenate([columns(i * group + j) for j in range(group)], axis=0)
            top = both.astype(jnp.bfloat16)
            at = pl.ds(pl.multiple_of(i * group * rows, group * rows), group * rows)
            pieces[at, : 2 * cols] = top
            pieces[at, 2 * cols :] = (both - top.astype(jnp.float32)).astype(jnp.bfloat16)

        def in_turn(k, _):
            arrive(k, 0)
            unpack((me + 2 * n - n // 2 - k) % n)
            return 0

        def in_order(i, _):
            unpack(i)
            return 0

        if group == 1:
            lax.fori_loop(0, n, in_turn, 0)
        else:
            lax.fori_loop(0, n, arrive, 0)
            lax.fori_loop(0, n // group, in_order, 0)

    def keep(panel):
        return (lattice[pl.ds(1 + panel, 1), :][:, :1] == band).astype(jnp.float32).astype(jnp.bfloat16)

    loads[0].wait()
    loads[1].wait()
    pl.semaphore_wait(barrier, n + 1)
    for i in range(3):
        at = pl.ds(pl.multiple_of(other_start + fetched[i] * part, part), part)
        masked[at, :] = masked[at, :] * keep(1 - core)
        sib_copy(i, fetched[i]).start()
    loads[2].wait()
    loads[3].wait()
    lax.fori_loop(0, n // 2, functools.partial(send, 0), 0)
    loads[4].wait()
    for i in range(3):
        sib_copy(i, fetched[i]).wait_recv()
        at = pl.ds(pl.multiple_of(own_start + fetched[i] * part, part), part)
        near = pl.ds(pl.multiple_of(fetched[i] * part, part), part)
        masked[at, :] = masked[at, :] * keep(core) + chip_sum[near, :]
        far_copy(i, fetched[i]).start()
    lax.fori_loop(n // 2, n, functools.partial(send, 0), 0)
    loads[5].wait()
    loads[6].wait()
    lax.fori_loop(0, n, functools.partial(send, 1), 0)
    for load in loads[7:]:
        load.wait()

    for i in range(3):
        far_copy(i, fetched[i]).wait_recv()
        at = pl.ds(pl.multiple_of(own_start + fetched[i] * part, part), part)
        near = pl.ds(pl.multiple_of(fetched[i] * part, part), part)
        vmat_ref[at, :] = masked[at, :] + far_sum[near, :]
        if i == 0:
            side_copy(fetched[0]).start()
        back_copy(i, own_start, fetched[i]).start()
    side_copy(fetched[0]).wait_send()
    side_copy(fetched[3]).wait_recv()
    back_copy(3, own_start, fetched[3]).start()

    receive(0, pieces0)
    for i in range(PARTS):
        back_copy(i, other_start, fetched[i]).wait_recv()
    store = pltpu.make_async_copy(vmat_ref, vmat_out, store_sem)
    store.start()
    def tile(j, _):
        at = pl.ds(pl.multiple_of(j * TILE, TILE), TILE)
        total = rotated(vmat_ref[:, at], pieces0[...])
        psi_sum[at, :] = (psi_sum[at, :].astype(jnp.float32) + total[:, :cols]).astype(jnp.bfloat16)
        hpsi_sum[at, :] = (hpsi_sum[at, :].astype(jnp.float32) + total[:, cols:]).astype(jnp.bfloat16)
        return 0

    lax.fori_loop(0, vmat_ref.shape[1] // TILE, tile, 0)

    receive(1, pieces1)
    for i in range(3):
        sib_copy(i, fetched[i]).wait_send()
        far_copy(i, fetched[i]).wait_send()
    for i in range(PARTS):
        back_copy(i, own_start, fetched[i]).wait_send()
    store.wait()


def exchange(n, keepers, res, loc, store, lattice, psi, hpsi):
    planes, rows, _, width = res.shape
    chunks = width // LANES
    depth, span = store.shape[1:]
    cols = width // n
    flat = (planes * rows * chunks, LANES)
    dma = pltpu.SemaphoreType.DMA
    hbm = pl.BlockSpec(memory_space=pltpu.HBM)
    parts = jax.ShapeDtypeStruct((depth, 4 * cols), jnp.bfloat16)
    plane = jax.ShapeDtypeStruct((span, cols), jnp.bfloat16)
    return pl.pallas_call(
        functools.partial(exchange_kernel, n, rows, chunks),
        out_shape=(
            jax.ShapeDtypeStruct((depth, span), jnp.bfloat16), parts, plane, plane, plane, plane,
        ),
        in_specs=[hbm] * 6,
        out_specs=(hbm,) + (pl.BlockSpec(memory_space=pltpu.VMEM),) * 5,
        scratch_shapes=[
            pltpu.VMEM((3, cols), jnp.int32),
            pltpu.VMEM(flat, jnp.float32),
            pltpu.VMEM(flat, jnp.float32),
            pltpu.VMEM((depth, span), jnp.bfloat16),
            pltpu.VMEM((depth, span), jnp.bfloat16),
            pltpu.VMEM((planes, n, 2 * rows, cols), jnp.int16),
            pltpu.VMEM((planes, n, 8, cols), jnp.float32),
            pltpu.VMEM((planes, n, 2 * rows, cols), jnp.int16),
            pltpu.VMEM((planes, n, 8, cols), jnp.float32),
            pltpu.VMEM((depth // 2, span), jnp.bfloat16),
            pltpu.VMEM((depth // 2, span), jnp.bfloat16),
            pltpu.VMEM((depth, 4 * cols), jnp.bfloat16),
            dma((11,)), dma, dma((planes, n)), dma((planes, n)), dma((planes, n)), dma((planes, n)),
            dma((3,)), dma((3,)), dma((3,)), dma((3,)), dma, dma,
            dma((PARTS,)), dma((PARTS,)),
        ],
        compiler_params=pltpu.CompilerParams(
            collective_id=0, has_side_effects=True, vmem_limit_bytes=GRANT
        ),
    )(
        jnp.concatenate([lattice, jnp.broadcast_to(keepers[:, None], (2, cols))], axis=0),
        res.reshape(flat), loc.reshape(flat), store.reshape(depth, span), psi, hpsi,
    )


def rotate_kernel(
    vmat_hbm, pieces, psi0, hpsi0, psi1, hpsi1, psi_out, hpsi_out,
    vmat, psi, hpsi, vmat_sem, psi_sem, hpsi_sem, first_sem,
):
    span, cols = psi.shape
    tiles = span // TILE
    first = (
        pltpu.make_async_copy(psi0, psi_out.at[0], first_sem.at[0]),
        pltpu.make_async_copy(hpsi0, hpsi_out.at[0], first_sem.at[1]),
    )
    loads = []
    for j in range(tiles):
        at = pl.ds(j * TILE, TILE)
        loads.append(pltpu.make_async_copy(vmat_hbm.at[:, at], vmat.at[:, at], vmat_sem.at[j]))
        loads[-1].start()
    for store in first:
        store.start()
    stores = []
    for j in range(tiles):
        at = pl.ds(j * TILE, TILE)
        loads[j].wait()
        total = rotated(vmat[:, at], pieces[...])
        psi[at, :] = (psi1[at, :].astype(jnp.float32) + total[:, :cols]).astype(jnp.bfloat16)
        hpsi[at, :] = (hpsi1[at, :].astype(jnp.float32) + total[:, cols:]).astype(jnp.bfloat16)
        stores += [
            pltpu.make_async_copy(psi.at[at], psi_out.at[1, at], psi_sem.at[j]),
            pltpu.make_async_copy(hpsi.at[at], hpsi_out.at[1, at], hpsi_sem.at[j]),
        ]
        for store in stores[-2:]:
            store.start()
    for store in stores:
        store.wait()
    for store in first:
        store.wait()


def rotate(vmat, pieces, psi0, hpsi0, psi1, hpsi1):
    span, cols = psi0.shape
    tiles = span // TILE
    dma = pltpu.SemaphoreType.DMA
    hbm = pl.BlockSpec(memory_space=pltpu.HBM)
    out = jax.ShapeDtypeStruct((2, span, cols), jnp.bfloat16)
    plane = pltpu.VMEM((span, cols), jnp.bfloat16)
    return pl.pallas_call(
        rotate_kernel,
        out_shape=(out, out),
        in_specs=[hbm] + [pl.BlockSpec(memory_space=pltpu.VMEM)] * 5,
        out_specs=(hbm, hbm),
        scratch_shapes=[
            pltpu.VMEM(vmat.shape, vmat.dtype), plane, plane,
            dma((tiles,)), dma((tiles,)), dma((tiles,)), dma((2,)),
        ],
        compiler_params=pltpu.CompilerParams(vmem_limit_bytes=GRANT),
    )(vmat, pieces, psi0, hpsi0, psi1, hpsi1)


def per_device(n, res, loc, psi, hpsi, store, keepers, lattice):
    planes, span, _, cols = psi.shape
    psi_in, hpsi_in = (x.reshape(planes, span, cols) for x in (psi, hpsi))
    handed = exchange(n, keepers, res, loc, store, lattice, psi_in, hpsi_in)
    psi_new, hpsi_new = rotate(*handed)
    return psi_new.reshape(psi.shape), hpsi_new.reshape(hpsi.shape)


def solution(mesh):
    in_specs = (
        P(None, "pw", "band", None),
        P(None, "pw", "band", None),
        P(None, None, "band", "pw"),
        P(None, None, "band", "pw"),
        P("band", None, None),
        P(),
        P("band", "pw"),
    )
    out_specs = (P(None, None, "band", "pw"), P(None, None, "band", "pw"))
    return jax.shard_map(
        functools.partial(per_device, mesh.shape["pw"]),
        mesh=mesh, in_specs=in_specs, out_specs=out_specs, check_vma=False,
    )
```
